128 devices in a mesh: rad: 8 (over y, core), lat: 16 (over x, z).
Axes of the slice: x: 4, y: 4, z: 4, core: 2. Of those that a mesh axis runs over, the one named last changes fastest.
Arguments:
- entropy: bfloat16 [256, 1024, 2, 256], P('lat', None, None, 'rad'), may hold values from -6 to 6
- legendre: bfloat16 [256, 1024, 1024], P('lat', 'rad'), may hold values from -0.1875 to 0.1875
- quad_weights: float32 [1024], replicated, may hold values from 0.5 to 2
- azimuthal_orders: int32 [256], replicated, may hold values from 0 to 1023, as said below
- azimuthal_flow: bfloat16 [3072, 256, 1024], P(None, 'lat', 'rad'), may hold values from -24 to 24
- radial_inverses: bfloat16 [1024, 256, 256], P(('rad', 'lat')), may hold values from -1 to 2
Outputs:
- entropy_next: bfloat16 [256, 1024, 2, 256], P(None, ('rad', 'lat'))
The draws below stay inside these ranges and needn't reach their ends.
Inputs may be any that keep to these rules, and one draw needn't show every extreme that they name: `azimuthal_orders`: distinct and ascending over the slots; the first is 0 and the last is 1023.
All inputs are finite; a program needn't handle non-finite values.
Results may differ from the reference program's by a relative error of at most 0.0051.
Values may be sent and summed in bfloat16 or wider, within the bound.
A program may use at most 128 MiB of HBM per device.

```python
import math
import jax
import jax.numpy as jnp
from jax import lax

L = 1024
NTH = 1024
NPHI = 3072
R = 256
MW = 256


def draw_azimuthal_orders(key, part):
    key = jax.random.fold_in(key, 7)
    inner = jax.random.permutation(key, L - 2)[:MW - 2].astype(jnp.int32) + 1
    chosen = jnp.concatenate([jnp.zeros((1,), jnp.int32), inner, jnp.full((1,), L - 1, jnp.int32)])
    return jnp.sort(chosen)


def draw_radial_inverses(key, part):
    key = jax.random.fold_in(key, 11)
    first_key, second_key = jax.random.split(key)
    diagonal = jax.random.uniform(first_key, (L, R), jnp.float32, 0.6, 1.4)
    spread = jnp.clip(jax.random.normal(second_key, (L, R, R), jnp.float32), -3.0, 3.0) * (0.5 / math.sqrt(R))
    identity = jnp.eye(R, dtype=jnp.float32)
    return (spread + identity[None, :, :] * diagonal[:, :, None]).astype(jnp.bfloat16)


def levels(key, shape, cuts, least, high):
    def one(axis_at, parts):
        draws = jax.random.uniform(jax.random.fold_in(jax.random.fold_in(key, 6), axis_at), (parts,), jnp.float32, least / len(cuts), high / len(cuts))
        return jnp.repeat(jnp.exp(draws), shape[axis_at] // parts).reshape((-1,) + (1,) * (len(shape) - axis_at - 1))

    level = one(*cuts[0])
    for cut in cuts[1:]:
        level = level * one(*cut)
    return level


def bell_draw(rng, dims, scale, reach, cuts=(), held_as=jnp.bfloat16):
    loudness = levels(rng, dims, cuts, -0.22, 0.18) if cuts else 1.0
    entries = jax.random.normal(rng, dims, jnp.float32) * scale * loudness
    return jnp.minimum(jnp.maximum(entries, -reach), reach).astype(held_as)


def setup_inputs(seed: int = 0) -> dict:
    splits = jax.random.split(jax.random.key(seed), 7)
    return {
        "entropy": bell_draw(splits[0], (MW, L, 2, R), 1.0, 6.0, ((0, 16), (3, 8))),
        "legendre": bell_draw(splits[1], (MW, NTH, L), L ** -0.5, 0.1875, ((0, 16), (1, 8))),
        "quad_weights": jnp.clip(jnp.exp(jax.random.uniform(splits[2], (NTH,), jnp.float32, math.log(0.5), math.log(2.0))), 0.5, 2.0),
        "azimuthal_orders": draw_azimuthal_orders(jax.random.fold_in(splits[6], 71), 0),
        "azimuthal_flow": bell_draw(splits[4], (NPHI, R, NTH), 4.0, 24.0, ((1, 16), (2, 8))),
        "radial_inverses": draw_radial_inverses(jax.random.fold_in(splits[6], 71), 0),
    }


def azimuth_tables(orders, n_phi, n_deg):
    steps_k = lax.broadcasted_iota(jnp.int32, (n_phi, 1), 0)
    phases = (steps_k * orders[None, :]) % n_phi
    angles = phases.astype(jnp.float32) * (2.0 * math.pi / n_phi)
    scaled = orders.astype(jnp.float32)[None, :] / n_deg
    sines = jnp.sin(angles)
    cosines = jnp.cos(angles)
    slope_table = jnp.stack([-(scaled * sines), -(scaled * cosines)], axis=2).astype(jnp.bfloat16)
    fourier_table = jnp.stack([cosines, -sines], axis=2).astype(jnp.bfloat16)
    return slope_table, fourier_table


def reference(entropy, legendre, quad_weights, azimuthal_orders, azimuthal_flow, radial_inverses):
    degrees = jnp.arange(L, dtype=jnp.int32)

    def synthesize_one(operands):
        table, coeffs, order = operands
        keep = degrees[None, :] >= order
        masked = jnp.where(keep, table, jnp.zeros_like(table))
        flattened = coeffs.reshape(L, 2 * R)
        return jnp.dot(flattened.T, masked.T, preferred_element_type=jnp.float32).astype(jnp.bfloat16)

    grid_values = lax.map(synthesize_one, (legendre, entropy, azimuthal_orders)).reshape(MW, 2, R, NTH)
    slope_table, fourier_table = azimuth_tables(azimuthal_orders, NPHI, L)
    slope_wide = slope_table.astype(jnp.float32)
    fourier_wide = fourier_table.astype(jnp.float32)

    def one_radius(radius):
        field = lax.dynamic_index_in_dim(grid_values, radius, 2, keepdims=False).astype(jnp.float32)
        flow_slice = lax.dynamic_index_in_dim(azimuthal_flow, radius, 1, keepdims=False).astype(jnp.float32)
        slope = jnp.einsum("kmc,mct->kt", slope_wide, field)
        forcing = (-flow_slice * slope).astype(jnp.bfloat16)
        forcing = lax.optimization_barrier(forcing).astype(jnp.float32)
        meridional = jnp.einsum("kmc,kt->mct", fourier_wide, forcing)
        return ((2.0 / NPHI) * meridional).astype(jnp.bfloat16)

    meridional = lax.map(one_radius, jnp.arange(R, dtype=jnp.int32))
    meridional = jnp.transpose(meridional, (1, 2, 0, 3))

    def analyze_one(operands):
        table, field, coeffs, order = operands
        keep = degrees[None, :] >= order
        weighted = jnp.where(keep, table.astype(jnp.float32) * quad_weights[:, None], 0.0).astype(jnp.bfloat16)
        product = jnp.dot(weighted.T, field.reshape(2 * R, NTH).T, preferred_element_type=jnp.float32)
        return (coeffs.reshape(L, 2 * R).astype(jnp.float32) + product).astype(jnp.bfloat16)

    right_side = lax.map(analyze_one, (legendre, meridional, entropy, azimuthal_orders)).reshape(MW, L, 2, R)
    updated = jnp.einsum("mlcs,lrs->mlcr", right_side.astype(jnp.float32), radial_inverses.astype(jnp.float32))
    return updated.astype(jnp.bfloat16)
```

```python
import math

import jax
import jax.numpy as jnp
from jax import lax
from jax.experimental import pallas as pl
from jax.experimental.pallas import tpu as pltpu
from jax.sharding import PartitionSpec as P

MESH = pl.DeviceIdType.MESH
F32, BF16 = jnp.float32, jnp.bfloat16
N_DEG = 1024
N_PHI = 3072
PEERS = 32
NT = (((1,), (1,)), ((), ()))
KB = 512


def wait_bytes(ref, sem):
    pltpu.make_async_copy(ref, ref, sem).wait()


def kernel(
    ent, leg, qw, orders, ta, tb, scaled, ua, ub, flow, out,
    ef, lg, wt, slope_t, fourier_t, fl, gsend, grecv, msend, mrecv, mx, wide, macc,
    r1send, r1recv, r2send, r2recv, fsend,
    ag_send, ag_recv, lg_send, lg_recv, fl_sem, g_send, g_recv, m_send, m_recv,
    r1_ssem, r1_rsem, r2_ssem, r2_rsem, f_send, f_recv,
):
    rad = lax.axis_index("rad")
    lat = lax.axis_index("lat")
    y, c = rad // 2, rad % 2
    me = 2 * lat + c
    up, down, across = (y + 1) % 4, (y + 3) % 4, (y + 2) % 4

    def place(index):
        return (2 * y + index % 2, index // 2)

    def flow_copy(step, buf):
        return pltpu.make_async_copy(flow.at[pl.ds(2 * step, 2)], fl.at[buf], fl_sem.at[buf])

    flow_copy(0, 0).start()
    flow_copy(1, 1).start()

    barrier = pltpu.get_barrier_semaphore()

    def greet(offset, carry):
        pl.semaphore_signal(
            barrier, inc=1, device_id=place((me + offset) % PEERS), device_id_type=MESH
        )
        return carry

    lax.fori_loop(1, PEERS, greet, 0)
    for row in (up, down):
        for core in range(2):
            pl.semaphore_signal(
                barrier, inc=1, device_id=(2 * row + core, lat), device_id_type=MESH
            )
    pl.semaphore_wait(barrier, PEERS - 1 + 4)

    def remote(src, dst, send_sem, recv_sem, device):
        pltpu.make_async_remote_copy(
            src_ref=src, dst_ref=dst, send_sem=send_sem, recv_sem=recv_sem,
            device_id=device, device_id_type=MESH,
        ).start()

    def all_to_all(source, target, send_sem, recv_sem):
        pltpu.make_async_copy(source(me), target, recv_sem).start()

        def send(offset, carry):
            dest = (me + offset) % PEERS
            remote(source(dest), target, send_sem, recv_sem, place(dest))
            return carry

        lax.fori_loop(1, PEERS, send, 0)

    def gather_direct(j):
        for row in (up, down):
            for core in range(2):
                remote(
                    ent.at[j, pl.ds(8 * core, 8)], ef.at[j, rad],
                    ag_send.at[j], ag_recv.at[j, rad], (2 * row + core, lat),
                )
        remote(
            ent.at[j, pl.ds(8 * (1 - c), 8)], ef.at[j, rad],
            ag_send.at[j], ag_recv.at[j, rad], (2 * y + 1 - c, lat),
        )
        pltpu.make_async_copy(ent.at[j, pl.ds(8 * c, 8)], ef.at[j, rad], ag_recv.at[j, rad]).start()

    def gather_wait(j, block):
        wait_bytes(ef.at[j, block], ag_recv.at[j, block])

    def gather_forward(j):
        for block, row in ((2 * down, up), (2 * up + 1, down)):
            gather_wait(j, block)
            remote(
                ef.at[j, block], ef.at[j, block],
                ag_send.at[j], ag_recv.at[j, block], (2 * row + c, lat),
            )

    def gather_rest(j):
        for block in (rad, 2 * y + 1 - c, 2 * down + 1, 2 * up, 2 * across, 2 * across + 1):
            gather_wait(j, block)

    def slope_rows(a, carry):
        cos_a, sin_a = ta[0, pl.ds(a, 1), :], ta[1, pl.ds(a, 1), :]
        sines = sin_a * tb[0] + cos_a * tb[1]
        slope_t[pl.ds(pl.multiple_of(64 * a, 64), 64), :] = (-(scaled[...] * sines)).astype(BF16)
        return carry

    def fourier_rows(block, carry):
        rows = pl.ds(pl.multiple_of(64 * block, 64), 64)
        cos_b, sin_b = ub[0, rows, :], ub[1, rows, :]
        for a in range(N_PHI // 128):
            cos_a, sin_a = ua[0, rows, a : a + 1], ua[1, rows, a : a + 1]
            fourier_t[rows, 128 * a : 128 * a + 128] = (cos_a * cos_b - sin_a * sin_b).astype(BF16)
        return carry

    def tables(slot, carry):
        order = orders[16 * lat + 8 * c + slot]
        table = lg[slot]
        degrees = lax.broadcasted_iota(jnp.int32, table.shape, 1)
        lg[slot] = jnp.where(degrees >= order, table, jnp.zeros_like(table))
        turned = jnp.transpose(table.astype(F32))
        weighted = turned * qw[pl.ds(y, 1), :]
        degrees = lax.broadcasted_iota(jnp.int32, turned.shape, 0)
        wt[slot] = jnp.where(degrees >= order, weighted, 0.0).astype(BF16)
        return carry

    def synthesize(j):
        def one(slot, carry):
            coeffs = ef[j, :, slot].reshape(256, N_DEG)
            values = lax.dot_general(coeffs, lg[slot], NT, preferred_element_type=F32)
            for p in range(16):
                for part in range(2):
                    at = 32 * (p // 2) + 16 * part + 8 * (p % 2)
                    for core in range(2):
                        wide[2 * p + core, pl.ds(8 * part + slot, 8, stride=16), :] = values[
                            at : at + 8, 128 * core : 128 * core + 128
                        ]
            return carry

        lax.fori_loop(0, 8, one, 0)

        def pack(dest, carry):
            gsend[j, dest] = wide[dest].astype(BF16).reshape(8, 16, 128)
            return carry

        lax.fori_loop(0, PEERS, pack, 0)
        all_to_all(
            lambda dest: gsend.at[j, dest], grecv.at[j, :, pl.ds(16 * me, 16), :],
            g_send.at[j], g_recv.at[j],
        )

    def grid(j):
        wait_bytes(grecv.at[j], g_recv.at[j])

        def pair(ip, carry):
            step = 4 * j + ip
            buf = ip % 2
            flow_copy(step, buf).wait()
            macc[...] = jnp.zeros_like(macc)

            def longitudes(kb, inner):
                rows = pl.ds(pl.multiple_of(KB * kb, KB), KB)
                points = jnp.concatenate([grecv[j, 2 * ip], grecv[j, 2 * ip + 1]], axis=1)
                slope = jnp.dot(slope_t[rows, :], points, preferred_element_type=F32)
                speed = jnp.concatenate([fl[buf, 0, rows, :], fl[buf, 1, rows, :]], axis=1)
                forcing = (-speed.astype(F32) * slope).astype(BF16)
                macc[...] += jnp.dot(fourier_t[:, rows], forcing, preferred_element_type=F32)
                return inner

            lax.fori_loop(0, N_PHI // KB, longitudes, 0)

            @pl.when(step < 6)
            def _():
                flow_copy(step + 2, buf).start()

            done = (macc[...] * (2.0 / N_PHI)).astype(BF16)
            for half in range(2):
                msend[j, :, 2 * ip + half] = done[:, 128 * half : 128 * half + 128].reshape(
                    PEERS, 16, 128
                )
            return carry

        lax.fori_loop(0, 4, pair, 0)
        all_to_all(
            lambda dest: msend.at[j, dest], mrecv.at[j, me], m_send.at[j], m_recv.at[j]
        )

    def arrange(j):
        wait_bytes(mrecv.at[j], m_recv.at[j])

        def unpack(src, carry):
            wide[src] = mrecv[j, src].reshape(128, 128).astype(F32)
            return carry

        lax.fori_loop(0, PEERS, unpack, 0)

        def one(slot, carry):
            for part in range(2):
                for p in range(0, 16, 2):
                    tiles = [
                        [
                            wide[2 * (p + q) + core, pl.ds(8 * part + slot, 8, stride=16), :]
                            for core in range(2)
                        ]
                        for q in range(2)
                    ]
                    block = jnp.concatenate(
                        [jnp.concatenate(pieces, axis=1) for pieces in tiles], axis=0
                    )
                    at = 128 * part + 8 * p
                    mx[j, slot, at : at + 16, :] = block.astype(BF16)
            return carry

        lax.fori_loop(0, 8, one, 0)

    def partial(j, slot, quarter):
        rows = pl.ds(pl.multiple_of(256 * quarter, 256), 256)
        return lax.dot_general(wt[slot, rows, :], mx[j, slot], NT, preferred_element_type=F32)

    def reduce_first(j):
        def far(slot, carry):
            r1send[j, slot] = partial(j, slot, across).astype(BF16)
            return carry

        for half, row in ((0, up), (1, down)):
            lax.fori_loop(4 * half, 4 * half + 4, far, 0)
            span = pl.ds(4 * half, 4)
            remote(
                r1send.at[j, span], r1recv.at[j, span],
                r1_ssem.at[j], r1_rsem.at[j, half], (2 * row + c, lat),
            )
        for way, row, half in ((0, up, 1), (1, down, 0)):

            def near(slot, carry):
                r2send[j, way, slot] = partial(j, slot, row).astype(BF16)
                return carry

            lax.fori_loop(4 * half, 4 * half + 4, near, 0)
            reduce_send(j, way, row, half)

    def reduce_send(j, way, row, half):
        span = pl.ds(4 * half, 4)
        remote(
            r2send.at[j, way, span], r2recv.at[j, way, span],
            r2_ssem.at[j], r2_rsem.at[j, way, half], (2 * row + c, lat),
        )

    def reduce_second(j):
        for way, row, half in ((0, up, 0), (1, down, 1)):
            span = pl.ds(4 * half, 4)
            wait_bytes(r1recv.at[j, span], r1_rsem.at[j, half])

            def near(slot, carry):
                total = partial(j, slot, row) + r1recv[j, slot].astype(F32)
                r2send[j, way, slot] = total.astype(BF16)
                return carry

            lax.fori_loop(4 * half, 4 * half + 4, near, 0)
            reduce_send(j, way, row, half)

    def finish(j):
        for way in range(2):
            for half in range(2):
                span = pl.ds(4 * half, 4)
                wait_bytes(r2recv.at[j, way, span], r2_rsem.at[j, way, half])
        lanes = pl.ds(pl.multiple_of(256 * y, 256), 256)
        eye = (
            lax.broadcasted_iota(jnp.int32, (256, 256), 0)
            == lax.broadcasted_iota(jnp.int32, (256, 256), 1)
        ).astype(F32).astype(BF16)

        def pair(index, carry):
            sides = []
            for u in range(2):
                slot = 2 * index + u
                own = ef[j, :, slot, :, lanes].reshape(8, 2, 16, 256)
                own = jnp.concatenate([own[:, 0], own[:, 1]], axis=0).reshape(256, 256)
                total = partial(j, slot, y) + lax.dot_general(
                    eye, own, NT, preferred_element_type=F32
                )
                total += r2recv[j, 0, slot].astype(F32) + r2recv[j, 1, slot].astype(F32)
                sides.append(total.reshape(PEERS, 8, 256))
            both = jnp.concatenate(sides, axis=1).astype(BF16)
            fsend[j, :, pl.ds(pl.multiple_of(16 * index, 16), 16), :] = both
            return carry

        lax.fori_loop(0, 4, pair, 0)
        all_to_all(
            lambda dest: fsend.at[j, 16 * (dest % 2) + dest // 2], out.at[j, me],
            f_send.at[j], f_recv.at[j],
        )

    gather_direct(0)
    mine = pl.ds(pl.multiple_of(128 * c, 128), 128)
    remote(
        leg.at[pl.ds(8 * (1 - c), 8)], lg.at[:, mine, :], lg_send, lg_recv, (2 * y + 1 - c, lat)
    )
    pltpu.make_async_copy(leg.at[pl.ds(8 * c, 8)], lg.at[:, mine, :], lg_recv).start()
    lax.fori_loop(0, N_PHI // 64, slope_rows, 0)
    gather_forward(0)
    gather_direct(1)
    lax.fori_loop(0, 8, fourier_rows, 0)
    wait_bytes(lg, lg_recv)
    lax.fori_loop(0, 8, tables, 0)
    gather_rest(0)
    synthesize(0)
    gather_forward(1)
    grid(0)
    gather_rest(1)
    synthesize(1)
    arrange(0)
    reduce_first(0)
    grid(1)
    reduce_second(0)
    arrange(1)
    reduce_first(1)
    finish(0)
    reduce_second(1)
    finish(1)
    for j in range(2):
        wait_bytes(out.at[j], f_recv.at[j])
    for j in range(2):
        wait_bytes(ef.at[j, pl.ds(0, 7)], ag_send.at[j])
        wait_bytes(gsend.at[j, pl.ds(0, PEERS - 1)], g_send.at[j])
        wait_bytes(msend.at[j, pl.ds(0, PEERS - 1)], m_send.at[j])
        wait_bytes(r1send.at[j], r1_ssem.at[j])
        wait_bytes(r2send.at[j], r2_ssem.at[j])
        wait_bytes(fsend.at[j, pl.ds(0, PEERS - 1)], f_send.at[j])
    wait_bytes(lg.at[:, pl.ds(0, 128), :], lg_send)


def waves(phases):
    angles = phases.astype(F32) * (2.0 * math.pi / N_PHI)
    return jnp.stack([jnp.cos(angles), jnp.sin(angles)])


def shards(entropy, legendre, quad_weights, azimuthal_orders, azimuthal_flow, radial_inverses):
    ent = jnp.transpose(entropy, (0, 2, 3, 1)).reshape(16, 2, 2, 2, 8, N_DEG)
    ent = jnp.transpose(ent, (3, 0, 1, 2, 4, 5)).reshape(2, 16, 32, N_DEG)
    flow = jnp.transpose(azimuthal_flow, (1, 0, 2))
    m = jnp.broadcast_to(azimuthal_orders.reshape(PEERS, 1, 8), (PEERS, 2, 8)).reshape(512)
    quarter = jnp.broadcast_to(
        (jnp.arange(2, dtype=jnp.int32) * (N_PHI // 4)).reshape(1, 2, 1), (PEERS, 2, 8)
    ).reshape(512)
    steps = lambda n: jnp.arange(n, dtype=jnp.int32)
    ta = waves((steps(48)[:, None] * 64 * m[None, :] + quarter[None, :]) % N_PHI)
    tb = waves((steps(64)[:, None] * m[None, :]) % N_PHI)
    ua = waves((steps(24)[None, :] * 128 * m[:, None] + quarter[:, None]) % N_PHI)
    ub = waves((steps(128)[None, :] * m[:, None]) % N_PHI)
    scaled = (m.astype(F32) / N_DEG).reshape(1, 512)
    hbm = pl.BlockSpec(memory_space=pl.ANY)
    vmem = pl.BlockSpec(memory_space=pltpu.VMEM)
    smem = pl.BlockSpec(memory_space=pltpu.SMEM)
    dma = pltpu.SemaphoreType.DMA
    received = pl.pallas_call(
        kernel,
        out_shape=jax.ShapeDtypeStruct((2, PEERS, 64, 256), BF16),
        in_specs=[hbm, hbm, vmem, smem, vmem, vmem, vmem, vmem, vmem, hbm],
        out_specs=hbm,
        scratch_shapes=[
            pltpu.VMEM((2, 8, 8, 32, N_DEG), BF16),
            pltpu.VMEM((8, 256, N_DEG), BF16),
            pltpu.VMEM((8, N_DEG, 256), BF16),
            pltpu.VMEM((N_PHI, 512), BF16),
            pltpu.VMEM((512, N_PHI), BF16),
            pltpu.VMEM((2, 2, N_PHI, 128), BF16),
            pltpu.VMEM((2, PEERS, 8, 16, 128), BF16),
            pltpu.VMEM((2, 8, 512, 128), BF16),
            pltpu.VMEM((2, PEERS, 8, 16, 128), BF16),
            pltpu.VMEM((2, PEERS, 8, 16, 128), BF16),
            pltpu.VMEM((2, 8, 256, 256), BF16),
            pltpu.VMEM((PEERS, 128, 128), F32),
            pltpu.VMEM((512, 256), F32),
            pltpu.VMEM((2, 8, 256, 256), BF16),
            pltpu.VMEM((2, 8, 256, 256), BF16),
            pltpu.VMEM((2, 2, 8, 256, 256), BF16),
            pltpu.VMEM((2, 2, 8, 256, 256), BF16),
            pltpu.VMEM((2, PEERS, 64, 256), BF16),
            dma((2,)), dma((2, 8)), dma, dma, dma((2,)),
            dma((2,)), dma((2,)), dma((2,)), dma((2,)),
            dma((2,)), dma((2, 2)), dma((2,)), dma((2, 2, 2)), dma((2,)), dma((2,)),
        ],
        compiler_params=pltpu.CompilerParams(
            collective_id=0, has_side_effects=True, vmem_limit_bytes=62 * 1024 * 1024
        ),
        cost_estimate=pl.CostEstimate(
            flops=17_000_000_000, bytes_accessed=24_000_000, transcendentals=0
        ),
    )(ent, legendre, quad_weights.reshape(4, 256), azimuthal_orders, ta, tb, scaled, ua, ub, flow)
    sides = received.reshape(2, 256, 8, 2, 128)
    inverses = jnp.transpose(radial_inverses.reshape(8, 256, 16, 2, 8), (0, 3, 2, 4, 1))
    inverses = inverses.reshape(8, 2, 128, 256)
    updated = jnp.einsum("jslcq,ljqr->slcr", sides, inverses, preferred_element_type=F32)
    return updated.astype(BF16)


def solution(mesh):
    placed = (
        P("lat", None, None, "rad"),
        P("lat", "rad", None),
        P(),
        P(),
        P(None, "lat", "rad"),
        P(("rad", "lat"), None, None),
    )
    return jax.shard_map(
        shards,
        mesh=mesh,
        in_specs=placed,
        out_specs=P(None, ("rad", "lat"), None, None),
        check_vma=False,
    )
```

```python
import math

import jax
import jax.numpy as jnp
from jax import lax
from jax.experimental import pallas as pl
from jax.experimental.pallas import tpu as pltpu
from jax.sharding import PartitionSpec as P

MESH = pl.DeviceIdType.MESH
F32, BF16 = jnp.float32, jnp.bfloat16
N_DEG = 1024
N_PHI = 3072
PEERS = 32
CHUNKS = 4
NT = (((1,), (1,)), ((), ()))
KB = 512
FB = 128


def wait_bytes(ref, sem):
    pltpu.make_async_copy(ref, ref, sem).wait()


def waves(product):
    turns = jnp.floor(product * (4.0 / N_PHI) + 0.5)
    x = (product - turns * (N_PHI // 4)) * (2.0 * math.pi / N_PHI)
    x2 = x * x
    sine = x * (1.0 + x2 * (-1 / 6 + x2 * (1 / 120 + x2 * (-1 / 5040 + x2 * (1 / 362880)))))
    cosine = 1.0 + x2 * (-0.5 + x2 * (1 / 24 + x2 * (-1 / 720 + x2 * (1 / 40320))))
    quarter = turns - 4.0 * jnp.floor(turns * 0.25)
    odd = (quarter == 1.0) | (quarter == 3.0)
    first = jnp.where(odd, sine, cosine)
    second = jnp.where(odd, cosine, sine)
    cos = jnp.where((quarter == 1.0) | (quarter == 2.0), -first, first)
    sin = jnp.where(quarter >= 2.0, -second, second)
    return cos, sin


def kernel(
    ent, leg, qw, orders, flow, out,
    ef, lg, wt, slope_t, fourier_t, fl, raw, tb, gsend, grecv, msend, mrecv, mx, wide, macc,
    r1send, r1recv, r2send, r2recv, fsend,
    ag_send, ag_recv, lg_send, lg_recv, raw_sem, g_send, g_recv, m_send, m_recv,
    r1_ssem, r1_rsem, r2_ssem, r2_rsem, f_send, f_recv,
):
    rad = lax.axis_index("rad")
    lat = lax.axis_index("lat")
    y, c = rad // 2, rad % 2
    me = 2 * lat + c
    up, down, across = (y + 1) % 4, (y + 3) % 4, (y + 2) % 4

    def place(index):
        return (2 * y + index % 2, index // 2)

    def raw_copy(block):
        rows = pl.ds(pl.multiple_of(FB * block, FB), FB)
        return pltpu.make_async_copy(flow.at[rows], raw.at[block % 2], raw_sem.at[block % 2])

    raw_copy(0).start()
    raw_copy(1).start()

    barrier = pltpu.get_barrier_semaphore()

    def greet(offset, carry):
        pl.semaphore_signal(
            barrier, inc=1, device_id=place((me + offset) % PEERS), device_id_type=MESH
        )
        return carry

    lax.fori_loop(1, PEERS, greet, 0)
    for row in (up, down):
        for core in range(2):
            pl.semaphore_signal(
                barrier, inc=1, device_id=(2 * row + core, lat), device_id_type=MESH
            )
    pl.semaphore_wait(barrier, PEERS - 1 + 4)

    def remote(src, dst, send_sem, recv_sem, device):
        pltpu.make_async_remote_copy(
            src_ref=src, dst_ref=dst, send_sem=send_sem, recv_sem=recv_sem,
            device_id=device, device_id_type=MESH,
        ).start()

    def all_to_all(source, target, send_sem, recv_sem):
        pltpu.make_async_copy(source(me), target, recv_sem).start()

        def send(offset, carry):
            dest = (me + offset) % PEERS
            remote(source(dest), target, send_sem, recv_sem, place(dest))
            return carry

        lax.fori_loop(1, PEERS, send, 0)

    def sent(buffer, sem):
        wait_bytes(buffer.at[pl.ds(0, PEERS - 1)], sem)

    def gather_direct(j):
        for row in (up, down):
            for core in range(2):
                remote(
                    ent.at[j, pl.ds(8 * core, 8)], ef.at[j, rad],
                    ag_send.at[j], ag_recv.at[j, rad], (2 * row + core, lat),
                )
        remote(
            ent.at[j, pl.ds(8 * (1 - c), 8)], ef.at[j, rad],
            ag_send.at[j], ag_recv.at[j, rad], (2 * y + 1 - c, lat),
        )
        pltpu.make_async_copy(ent.at[j, pl.ds(8 * c, 8)], ef.at[j, rad], ag_recv.at[j, rad]).start()

    def gather_wait(j, block):
        wait_bytes(ef.at[j, block], ag_recv.at[j, block])

    def gather_forward(j):
        for block, row in ((2 * down, up), (2 * up + 1, down)):
            gather_wait(j, block)
            remote(
                ef.at[j, block], ef.at[j, block],
                ag_send.at[j], ag_recv.at[j, block], (2 * row + c, lat),
            )

    def gather_rest(j):
        for block in (rad, 2 * y + 1 - c, 2 * down + 1, 2 * up, 2 * across, 2 * across + 1):
            gather_wait(j, block)

    columns = lax.broadcasted_iota(jnp.int32, (1, 512), 1)
    column_slots = (columns // 16) * 8 + columns % 8

    def column_order(slot, row):
        return jnp.where(column_slots == slot, orders[slot].astype(F32), row)

    def slope_rows(m_row):
        quarter = jnp.where(columns % 16 >= 8, N_PHI / 4, 0.0)
        cos_b, sin_b = waves(lax.broadcasted_iota(jnp.int32, (64, 512), 0).astype(F32) * m_row)
        tb[0] = cos_b
        tb[1] = sin_b
        scaled = m_row * (1.0 / N_DEG)

        def rows(a, carry):
            cos_a, sin_a = waves((64 * a).astype(F32) * m_row + quarter)
            sines = sin_a * tb[0] + cos_a * tb[1]
            slope_t[pl.ds(pl.multiple_of(64 * a, 64), 64), :] = (-(scaled * sines)).astype(BF16)
            return carry

        lax.fori_loop(0, N_PHI // 64, rows, 0)

    def fourier_rows(m_row):
        macc[:, :128] = jnp.transpose(jnp.broadcast_to(m_row, (128, 512)))
        lanes = lax.broadcasted_iota(jnp.int32, (64, 128), 1).astype(F32)
        second = lax.broadcasted_iota(jnp.int32, (64, 128), 0) % 16 >= 8
        quarter = jnp.where(second, N_PHI / 4, 0.0)

        def rows_of(block, carry):
            rows = pl.ds(pl.multiple_of(64 * block, 64), 64)
            m = macc[rows, :128]
            cos_b, sin_b = waves(lanes * m)
            cos_a, sin_a = waves(jnp.minimum(lanes, N_PHI // 128 - 1) * 128.0 * m + quarter)
            for a in range(N_PHI // 128):
                cosines = cos_a[:, a : a + 1] * cos_b - sin_a[:, a : a + 1] * sin_b
                fourier_t[rows, 128 * a : 128 * a + 128] = cosines.astype(BF16)
            return carry

        lax.fori_loop(0, 8, rows_of, 0)

    def turn_flow(block, carry):
        raw_copy(block).wait()
        piece = raw[block % 2].reshape(2, 64 * 16, 128)
        for half in range(2):
            wide[half] = piece[half].astype(F32)

        @pl.when(block + 2 < N_PHI // FB)
        def _():
            raw_copy(block + 2).start()

        for half in range(2):
            rows = pl.ds(pl.multiple_of(FB * block + 64 * half, 64), 64)
            for level in range(16):
                fl[level, rows, :] = wide[half, pl.ds(level, 64, stride=16), :].astype(BF16)
        return carry

    def tables(slot, carry):
        order = orders[16 * lat + 8 * c + slot]
        table = lg[slot]
        degrees = lax.broadcasted_iota(jnp.int32, table.shape, 1)
        lg[slot] = jnp.where(degrees >= order, table, jnp.zeros_like(table))
        turned = jnp.transpose(table.astype(F32))
        weights = jnp.concatenate([qw[pl.ds(2 * y, 1), :], qw[pl.ds(2 * y + 1, 1), :]], axis=1)
        weighted = turned * weights
        degrees = lax.broadcasted_iota(jnp.int32, turned.shape, 0)
        wt[slot] = jnp.where(degrees >= order, weighted, 0.0).astype(BF16)
        return carry

    def synthesize(j):
        gather_rest(j)

        def one(slot, carry):
            coeffs = ef[j, :, slot].reshape(128, N_DEG)
            values = lax.dot_general(coeffs, lg[slot], NT, preferred_element_type=F32)
            for block in range(8):
                for part in range(2):
                    at = 16 * block + 8 * part
                    for core in range(2):
                        wide[core, pl.ds(128 * block + 8 * part + slot, 8, stride=16), :] = values[
                            at : at + 8, 128 * core : 128 * core + 128
                        ]
            return carry

        lax.fori_loop(0, 8, one, 0)
        buf = j % 2
        if j >= 2:
            sent(gsend.at[buf], g_send.at[j - 2])

        def pack(p, carry):
            rows = pl.ds(pl.multiple_of(64 * p, 64), 64)
            for core in range(2):
                gsend[buf, 2 * p + core] = wide[core, rows, :].astype(BF16).reshape(4, 16, 128)
            return carry

        lax.fori_loop(0, 16, pack, 0)
        all_to_all(
            lambda dest: gsend.at[buf, dest], grecv.at[j, :, pl.ds(16 * me, 16), :],
            g_send.at[j], g_recv.at[j],
        )

    def grid(j):
        wait_bytes(grecv.at[j], g_recv.at[j])
        buf = j % 2
        if j >= 2:
            sent(msend.at[buf], m_send.at[j - 2])

        def pair(ip, carry):
            macc[...] = jnp.zeros_like(macc)

            def longitudes(kb, inner):
                rows = pl.ds(pl.multiple_of(KB * kb, KB), KB)
                points = jnp.concatenate([grecv[j, 2 * ip], grecv[j, 2 * ip + 1]], axis=1)
                slope = jnp.dot(slope_t[rows, :], points, preferred_element_type=F32)
                level = 4 * j + 2 * ip
                speed = jnp.concatenate([fl[level, rows, :], fl[level + 1, rows, :]], axis=1)
                forcing = (-speed.astype(F32) * slope).astype(BF16)
                macc[...] += jnp.dot(fourier_t[:, rows], forcing, preferred_element_type=F32)
                return inner

            lax.fori_loop(0, N_PHI // KB, longitudes, 0)
            done = (macc[...] * (2.0 / N_PHI)).astype(BF16)
            for half in range(2):
                msend[buf, :, 2 * ip + half] = done[:, 128 * half : 128 * half + 128].reshape(
                    PEERS, 16, 128
                )
            return carry

        lax.fori_loop(0, 2, pair, 0)
        all_to_all(
            lambda dest: msend.at[buf, dest], mrecv.at[j, me], m_send.at[j], m_recv.at[j]
        )

    def arrange(j):
        wait_bytes(mrecv.at[j], m_recv.at[j])

        def unpack(p, carry):
            rows = pl.ds(pl.multiple_of(64 * p, 64), 64)
            for core in range(2):
                wide[core, rows, :] = mrecv[j, 2 * p + core].reshape(64, 128).astype(F32)
            return carry

        lax.fori_loop(0, 16, unpack, 0)

        def one(slot, carry):
            for part in range(2):
                for block in range(0, 8, 2):
                    tiles = [
                        [
                            wide[core, pl.ds(128 * (block + q) + 8 * part + slot, 8, stride=16), :]
                            for core in range(2)
                        ]
                        for q in range(2)
                    ]
                    both = jnp.concatenate(
                        [jnp.concatenate(pieces, axis=1) for pieces in tiles], axis=0
                    )
                    at = 64 * part + 8 * block
                    mx[j, slot, at : at + 16, :] = both.astype(BF16)
            return carry

        lax.fori_loop(0, 8, one, 0)

    def partial(j, slot, quarter):
        rows = pl.ds(pl.multiple_of(256 * quarter, 256), 256)
        return lax.dot_general(wt[slot, rows, :], mx[j, slot], NT, preferred_element_type=F32)

    def reduce_first(j):
        buf = j % 2
        if j >= 2:
            wait_bytes(r1send.at[buf], r1_ssem.at[j - 2])
            wait_bytes(r2send.at[buf], r2_ssem.at[j - 2])

        def far(slot, carry):
            r1send[buf, slot] = partial(j, slot, across).astype(BF16)
            return carry

        for half, row in ((0, up), (1, down)):
            lax.fori_loop(4 * half, 4 * half + 4, far, 0)
            span = pl.ds(4 * half, 4)
            remote(
                r1send.at[buf, span], r1recv.at[j, span],
                r1_ssem.at[j], r1_rsem.at[j, half], (2 * row + c, lat),
            )
        for way, row, half in ((0, up, 1), (1, down, 0)):

            def near(slot, carry):
                r2send[buf, way, slot] = partial(j, slot, row).astype(BF16)
                return carry

            lax.fori_loop(4 * half, 4 * half + 4, near, 0)
            reduce_send(j, way, row, half)

    def reduce_send(j, way, row, half):
        span = pl.ds(4 * half, 4)
        remote(
            r2send.at[j % 2, way, span], r2recv.at[j, way, span],
            r2_ssem.at[j], r2_rsem.at[j, way, half], (2 * row + c, lat),
        )

    def reduce_second(j):
        for way, row, half in ((0, up, 0), (1, down, 1)):
            span = pl.ds(4 * half, 4)
            wait_bytes(r1recv.at[j, span], r1_rsem.at[j, half])

            def near(slot, carry):
                total = partial(j, slot, row) + r1recv[j, slot].astype(F32)
                r2send[j % 2, way, slot] = total.astype(BF16)
                return carry

            lax.fori_loop(4 * half, 4 * half + 4, near, 0)
            reduce_send(j, way, row, half)

    def finish(j):
        buf = j % 2
        for way in range(2):
            for half in range(2):
                span = pl.ds(4 * half, 4)
                wait_bytes(r2recv.at[j, way, span], r2_rsem.at[j, way, half])
        lanes = pl.ds(pl.multiple_of(256 * y, 256), 256)
        eye = (
            lax.broadcasted_iota(jnp.int32, (256, 256), 0)
            == lax.broadcasted_iota(jnp.int32, (256, 256), 1)
        ).astype(F32).astype(BF16)

        def one(slot, carry):
            own = ef[j, :, slot, :, lanes].astype(F32)
            own = jnp.concatenate([own[:, :8], own[:, 8:]], axis=0).reshape(128, 256)
            total = partial(j, slot, y) + lax.dot_general(
                eye, own.astype(BF16), NT, preferred_element_type=F32
            )
            total += r2recv[j, 0, slot].astype(F32) + r2recv[j, 1, slot].astype(F32)
            for core in range(2):
                for p in range(16):
                    at = 128 * core + 8 * p
                    wide[core, pl.ds(64 * p + slot, 8, stride=8), :] = total[at : at + 8]
            return carry

        lax.fori_loop(0, 8, one, 0)
        if j >= 2:
            sent(fsend.at[buf], f_send.at[j - 2])
            wait_bytes(out.at[j - 2], f_recv.at[j - 2])

        def pack(p, carry):
            rows = pl.ds(pl.multiple_of(64 * p, 64), 64)
            for core in range(2):
                fsend[buf, 2 * p + core] = wide[core, rows, :].astype(BF16)
            return carry

        lax.fori_loop(0, 16, pack, 0)
        all_to_all(lambda dest: fsend.at[buf, dest], out.at[j, me], f_send.at[j], f_recv.at[j])

    gather_direct(0)
    mine = pl.ds(pl.multiple_of(128 * c, 128), 128)
    remote(
        leg.at[pl.ds(8 * (1 - c), 8)], lg.at[:, mine, :], lg_send, lg_recv, (2 * y + 1 - c, lat)
    )
    pltpu.make_async_copy(leg.at[pl.ds(8 * c, 8)], lg.at[:, mine, :], lg_recv).start()
    m_row = lax.fori_loop(0, 256, column_order, jnp.zeros((1, 512), F32))
    slope_rows(m_row)
    fourier_rows(m_row)
    lax.fori_loop(0, 12, turn_flow, 0)
    gather_forward(0)
    gather_direct(1)
    gather_direct(2)
    lax.fori_loop(12, N_PHI // FB, turn_flow, 0)
    wait_bytes(lg, lg_recv)
    lax.fori_loop(0, 8, tables, 0)
    synthesize(0)
    gather_forward(1)
    gather_direct(3)
    grid(0)
    synthesize(1)
    gather_forward(2)
    arrange(0)
    reduce_first(0)
    grid(1)
    synthesize(2)
    gather_forward(3)
    reduce_second(0)
    arrange(1)
    reduce_first(1)
    grid(2)
    synthesize(3)
    finish(0)
    reduce_second(1)
    arrange(2)
    reduce_first(2)
    grid(3)
    finish(1)
    reduce_second(2)
    arrange(3)
    reduce_first(3)
    finish(2)
    reduce_second(3)
    finish(3)
    for j in range(CHUNKS):
        wait_bytes(ef.at[j, pl.ds(0, 7)], ag_send.at[j])
    for j in range(CHUNKS - 2, CHUNKS):
        sent(gsend.at[j % 2], g_send.at[j])
        sent(msend.at[j % 2], m_send.at[j])
        wait_bytes(r1send.at[j % 2], r1_ssem.at[j])
        wait_bytes(r2send.at[j % 2], r2_ssem.at[j])
        sent(fsend.at[j % 2], f_send.at[j])
        wait_bytes(out.at[j], f_recv.at[j])
    wait_bytes(lg.at[:, pl.ds(0, 128), :], lg_send)


def radial_kernel(sides, inverses, out):
    source = lax.broadcasted_iota(jnp.int32, (256, 512), 0)
    lane = lax.broadcasted_iota(jnp.int32, (256, 512), 1)
    chunk, rest = lane // 128, lane % 128
    level = (rest % 64) // 4 * 16 + chunk * 4 + rest % 4
    hits = (source == level).astype(F32)
    part = rest // 64

    def two_degrees(index, carry):
        rows = pl.ds(pl.multiple_of(16 * index, 16), 16)
        piece = sides[:, :, rows, :].astype(F32)
        for u in range(2):
            flat = piece[:, :, 8 * u : 8 * u + 8, :].reshape(CHUNKS, 256, 128).astype(BF16)
            left = jnp.concatenate([flat[j] for j in range(CHUNKS)], axis=1)
            inverse = inverses[2 * index + u]
            for half in range(2):
                spread = jnp.where(part == half, hits, 0.0).astype(BF16)
                right = jnp.dot(inverse, spread, preferred_element_type=F32).astype(BF16)
                out[2 * index + u, :, 256 * half : 256 * half + 256] = lax.dot_general(
                    left, right, NT, preferred_element_type=F32
                ).astype(BF16)
        return carry

    lax.fori_loop(0, 4, two_degrees, 0)


def shards(entropy, legendre, quad_weights, azimuthal_orders, azimuthal_flow, radial_inverses):
    ent = jnp.transpose(entropy, (0, 2, 3, 1)).reshape(16, 2, 2, CHUNKS, 4, N_DEG)
    ent = jnp.transpose(ent, (3, 0, 1, 2, 4, 5)).reshape(CHUNKS, 16, 16, N_DEG)
    hbm = pl.BlockSpec(memory_space=pl.ANY)
    vmem = pl.BlockSpec(memory_space=pltpu.VMEM)
    smem = pl.BlockSpec(memory_space=pltpu.SMEM)
    dma = pltpu.SemaphoreType.DMA
    received = pl.pallas_call(
        kernel,
        out_shape=jax.ShapeDtypeStruct((CHUNKS, PEERS, 64, 128), BF16),
        in_specs=[hbm, hbm, vmem, smem, hbm],
        out_specs=hbm,
        scratch_shapes=[
            pltpu.VMEM((CHUNKS, 8, 8, 16, N_DEG), BF16),
            pltpu.VMEM((8, 256, N_DEG), BF16),
            pltpu.VMEM((8, N_DEG, 256), BF16),
            pltpu.VMEM((N_PHI, 512), BF16),
            pltpu.VMEM((512, N_PHI), BF16),
            pltpu.VMEM((16, N_PHI, 128), BF16),
            pltpu.VMEM((2, FB, 16, 128), BF16),
            pltpu.VMEM((2, 64, 512), F32),
            pltpu.VMEM((2, PEERS, 4, 16, 128), BF16),
            pltpu.VMEM((CHUNKS, 4, 512, 128), BF16),
            pltpu.VMEM((2, PEERS, 4, 16, 128), BF16),
            pltpu.VMEM((CHUNKS, PEERS, 4, 16, 128), BF16),
            pltpu.VMEM((CHUNKS, 8, 128, 256), BF16),
            pltpu.VMEM((2, 1024, 128), F32),
            pltpu.VMEM((512, 256), F32),
            pltpu.VMEM((2, 8, 256, 128), BF16),
            pltpu.VMEM((CHUNKS, 8, 256, 128), BF16),
            pltpu.VMEM((2, 2, 8, 256, 128), BF16),
            pltpu.VMEM((CHUNKS, 2, 8, 256, 128), BF16),
            pltpu.VMEM((2, PEERS, 64, 128), BF16),
            dma((CHUNKS,)), dma((CHUNKS, 8)), dma, dma, dma((2,)),
            dma((CHUNKS,)), dma((CHUNKS,)), dma((CHUNKS,)), dma((CHUNKS,)),
            dma((CHUNKS,)), dma((CHUNKS, 2)), dma((CHUNKS,)), dma((CHUNKS, 2, 2)),
            dma((CHUNKS,)), dma((CHUNKS,)),
        ],
        compiler_params=pltpu.CompilerParams(
            collective_id=0, has_side_effects=True, vmem_limit_bytes=62 * 1024 * 1024
        ),
        cost_estimate=pl.CostEstimate(
            flops=17_000_000_000, bytes_accessed=24_000_000, transcendentals=0
        ),
    )(ent, legendre, quad_weights.reshape(8, 128), azimuthal_orders, azimuthal_flow)
    updated = pl.pallas_call(
        radial_kernel,
        out_shape=jax.ShapeDtypeStruct((8, 256, 512), BF16),
        in_specs=[vmem, vmem],
        out_specs=vmem,
        compiler_params=pltpu.CompilerParams(vmem_limit_bytes=32 * 1024 * 1024),
        cost_estimate=pl.CostEstimate(
            flops=3_200_000_000, bytes_accessed=6_000_000, transcendentals=0
        ),
    )(received, radial_inverses)
    return jnp.transpose(updated.reshape(8, 256, 2, 256), (1, 0, 2, 3))


def solution(mesh):
    placed = (
        P("lat", None, None, "rad"),
        P("lat", "rad", None),
        P(),
        P(),
        P(None, "lat", "rad"),
        P(("rad", "lat"), None, None),
    )
    return jax.shard_map(
        shards,
        mesh=mesh,
        in_specs=placed,
        out_specs=P(None, ("rad", "lat"), None, None),
        check_vma=False,
    )
```

```python
import math

import jax
import jax.numpy as jnp
from jax import lax
from jax.experimental import pallas as pl
from jax.experimental.pallas import tpu as pltpu
from jax.sharding import PartitionSpec as P

MESH = pl.DeviceIdType.MESH
F32, BF16 = jnp.float32, jnp.bfloat16
N_DEG = 1024
N_PHI = 3072
PEERS = 32
CHUNKS = 4
NT = (((1,), (1,)), ((), ()))
KB = 256
FB = 64


def wait_bytes(ref, sem):
    pltpu.make_async_copy(ref, ref, sem).wait()


def waves(product):
    turns = jnp.floor(product * (4.0 / N_PHI) + 0.5)
    x = (product - turns * (N_PHI // 4)) * (2.0 * math.pi / N_PHI)
    x2 = x * x
    sine = x * (1.0 + x2 * (-1 / 6 + x2 * (1 / 120 + x2 * (-1 / 5040 + x2 * (1 / 362880)))))
    cosine = 1.0 + x2 * (-0.5 + x2 * (1 / 24 + x2 * (-1 / 720 + x2 * (1 / 40320))))
    quarter = turns - 4.0 * jnp.floor(turns * 0.25)
    odd = (quarter == 1.0) | (quarter == 3.0)
    first = jnp.where(odd, sine, cosine)
    second = jnp.where(odd, cosine, sine)
    cos = jnp.where((quarter == 1.0) | (quarter == 2.0), -first, first)
    sin = jnp.where(quarter >= 2.0, -second, second)
    return cos, sin


def kernel(
    ent, leg, qw, orders, flow, inverses, out,
    er, inv, fr, ef, lg, wt, slope_t, fourier_t, fl, raw, tb, gsend, grecv, msend, mrecv, mx, wide, macc,
    r1send, r1recv, r2send, r2recv, fsend,
    ag_send, ag_recv, lg_send, lg_recv, raw_sem, g_send, g_recv, m_send, m_recv,
    r1_ssem, r1_rsem, r2_ssem, r2_rsem, f_send, f_recv, er_sem, inv_sem, out_sem,
):
    rad = lax.axis_index("rad")
    lat = lax.axis_index("lat")
    y, c = rad // 2, rad % 2
    me = 2 * lat + c
    up, down, across = (y + 1) % 4, (y + 3) % 4, (y + 2) % 4

    def place(index):
        return (2 * y + index % 2, index // 2)

    def raw_copy(block):
        rows = pl.ds(pl.multiple_of(FB * block, FB), FB)
        return pltpu.make_async_copy(flow.at[rows], raw.at[block % 2], raw_sem.at[block % 2])

    own_rows = pltpu.make_async_copy(ent, er, er_sem)
    own_rows.start()
    raw_copy(0).start()
    raw_copy(1).start()
    own_inverses = pltpu.make_async_copy(inverses, inv, inv_sem)
    own_inverses.start()

    barrier = pltpu.get_barrier_semaphore()

    def greet(offset, carry):
        pl.semaphore_signal(
            barrier, inc=1, device_id=place((me + offset) % PEERS), device_id_type=MESH
        )
        return carry

    lax.fori_loop(1, PEERS, greet, 0)
    for row in (up, down):
        for core in range(2):
            pl.semaphore_signal(
                barrier, inc=1, device_id=(2 * row + core, lat), device_id_type=MESH
            )

    def regroup(slot, carry):
        rows = er[slot].astype(F32).reshape(4, 16, N_DEG)
        low = lax.broadcasted_iota(jnp.int32, (8, N_DEG), 0) < 4
        for j in range(CHUNKS):
            tiles = []
            for part in range(2):
                first = rows[2 * part, 8 * (j // 2) : 8 * (j // 2) + 8]
                second = rows[2 * part + 1, 8 * (j // 2) : 8 * (j // 2) + 8]
                if j % 2 == 0:
                    tiles.append(jnp.where(low, first, pltpu.roll(second, 4, axis=0)))
                else:
                    tiles.append(jnp.where(low, pltpu.roll(first, 4, axis=0), second))
            er[slot, 16 * j : 16 * j + 16, :] = jnp.concatenate(tiles, axis=0).astype(BF16)
        return carry

    own_rows.wait()
    lax.fori_loop(0, 16, regroup, 0)
    pl.semaphore_wait(barrier, PEERS - 1 + 4)

    def remote(src, dst, send_sem, recv_sem, device):
        pltpu.make_async_remote_copy(
            src_ref=src, dst_ref=dst, send_sem=send_sem, recv_sem=recv_sem,
            device_id=device, device_id_type=MESH,
        ).start()

    def all_to_all(source, target, send_sem, recv_sem):
        pltpu.make_async_copy(source(me), target, recv_sem).start()

        def send(offset, carry):
            dest = (me + offset) % PEERS
            remote(source(dest), target, send_sem, recv_sem, place(dest))
            return carry

        lax.fori_loop(1, PEERS, send, 0)

    def sent(buffer, sem):
        wait_bytes(buffer.at[pl.ds(0, PEERS - 1)], sem)

    def gather_direct(j):
        rows = pl.ds(16 * j, 16)
        for row in (up, down):
            for core in range(2):
                remote(
                    er.at[pl.ds(8 * core, 8), rows, :], ef.at[j, rad],
                    ag_send.at[j], ag_recv.at[j, rad], (2 * row + core, lat),
                )
        remote(
            er.at[pl.ds(8 * (1 - c), 8), rows, :], ef.at[j, rad],
            ag_send.at[j], ag_recv.at[j, rad], (2 * y + 1 - c, lat),
        )
        pltpu.make_async_copy(
            er.at[pl.ds(8 * c, 8), rows, :], ef.at[j, rad], ag_recv.at[j, rad]
        ).start()

    def gather_wait(j, block):
        wait_bytes(ef.at[j, block], ag_recv.at[j, block])

    def gather_forward(j):
        for block, row in ((2 * down, up), (2 * up + 1, down)):
            gather_wait(j, block)
            remote(
                ef.at[j, block], ef.at[j, block],
                ag_send.at[j], ag_recv.at[j, block], (2 * row + c, lat),
            )

    def gather_rest(j):
        for block in (rad, 2 * y + 1 - c, 2 * down + 1, 2 * up, 2 * across, 2 * across + 1):
            gather_wait(j, block)

    columns = lax.broadcasted_iota(jnp.int32, (1, 512), 1)
    column_slots = (columns // 16) * 8 + columns % 8

    def column_order(slot, row):
        return jnp.where(column_slots == slot, orders[slot].astype(F32), row)

    def slope_rows(m_row):
        quarter = jnp.where(columns % 16 >= 8, N_PHI / 4, 0.0)
        cos_b, sin_b = waves(lax.broadcasted_iota(jnp.int32, (64, 512), 0).astype(F32) * m_row)
        tb[0] = cos_b
        tb[1] = sin_b
        scaled = m_row * (1.0 / N_DEG)

        def rows(a, carry):
            cos_a, sin_a = waves((64 * a).astype(F32) * m_row + quarter)
            sines = sin_a * tb[0] + cos_a * tb[1]
            slope_t[pl.ds(pl.multiple_of(64 * a, 64), 64), :] = (-(scaled * sines)).astype(BF16)
            return carry

        lax.fori_loop(0, N_PHI // 64, rows, 0)

    def fourier_rows(m_row):
        macc[:, :128] = jnp.transpose(jnp.broadcast_to(m_row, (128, 512)))
        lanes = lax.broadcasted_iota(jnp.int32, (64, 128), 1).astype(F32)
        second = lax.broadcasted_iota(jnp.int32, (64, 128), 0) % 16 >= 8
        quarter = jnp.where(second, N_PHI / 4, 0.0)

        def rows_of(block, carry):
            rows = pl.ds(pl.multiple_of(64 * block, 64), 64)
            m = macc[rows, :128]
            cos_b, sin_b = waves(lanes * m)
            cos_a, sin_a = waves(jnp.minimum(lanes, N_PHI // 128 - 1) * 128.0 * m + quarter)
            for a in range(N_PHI // 128):
                cosines = cos_a[:, a : a + 1] * cos_b - sin_a[:, a : a + 1] * sin_b
                fourier_t[rows, 128 * a : 128 * a + 128] = cosines.astype(BF16)
            return carry

        lax.fori_loop(0, 8, rows_of, 0)

    def turn_flow(block, carry):
        raw_copy(block).wait()
        piece = raw[block % 2].reshape(2, FB * 8, 128)
        for half in range(2):
            wide[half, : FB * 8, :] = piece[half].astype(F32)

        @pl.when(block + 2 < N_PHI // FB)
        def _():
            raw_copy(block + 2).start()

        for half in range(2):
            rows = pl.ds(pl.multiple_of(FB * block + FB // 2 * half, FB // 2), FB // 2)
            for level in range(16):
                fl[level, rows, :] = wide[half, pl.ds(level, FB // 2, stride=16), :].astype(BF16)
        return carry

    def mask(slot, carry):
        order = orders[16 * lat + 8 * c + slot]
        table = lg[slot]
        degrees = lax.broadcasted_iota(jnp.int32, table.shape, 1)
        lg[slot] = jnp.where(degrees >= order, table, jnp.zeros_like(table))
        return carry

    def weigh(slot, carry):
        weights = jnp.concatenate([qw[pl.ds(2 * y, 1), :], qw[pl.ds(2 * y + 1, 1), :]], axis=1)
        weighted = (jnp.transpose(lg[slot].astype(F32)) * weights).astype(BF16)
        for quarter in range(4):
            rows = pl.ds(pl.multiple_of(256 * ((quarter - y + 4) % 4), 256), 256)
            wt[slot, rows, :] = weighted[256 * quarter : 256 * quarter + 256]
        return carry

    def synthesize(j):
        gather_rest(j)

        def one(slot, carry):
            coeffs = ef[j, :, slot].reshape(128, N_DEG)
            values = lax.dot_general(coeffs, lg[slot], NT, preferred_element_type=F32)
            for block in range(8):
                for part in range(2):
                    at = 16 * block + 8 * part
                    for core in range(2):
                        wide[core, pl.ds(128 * block + 8 * part + slot, 8, stride=16), :] = values[
                            at : at + 8, 128 * core : 128 * core + 128
                        ]
            return carry

        lax.fori_loop(0, 8, one, 0)
        buf = j % 2
        if j >= 2:
            sent(gsend.at[buf], g_send.at[j - 2])

        def pack(p, carry):
            rows = pl.ds(pl.multiple_of(64 * p, 64), 64)
            for core in range(2):
                gsend[buf, 2 * p + core] = wide[core, rows, :].astype(BF16).reshape(4, 16, 128)
            return carry

        lax.fori_loop(0, 16, pack, 0)
        all_to_all(
            lambda dest: gsend.at[buf, dest], grecv.at[j, :, pl.ds(16 * me, 16), :],
            g_send.at[j], g_recv.at[j],
        )

    def grid(j):
        wait_bytes(grecv.at[j], g_recv.at[j])
        buf = j % 2
        if j >= 2:
            sent(msend.at[buf], m_send.at[j - 2])

        macc[...] = jnp.zeros_like(macc)

        def longitudes(kb, carry):
            rows = pl.ds(pl.multiple_of(KB * kb, KB), KB)
            points = jnp.concatenate([grecv[j, i] for i in range(4)], axis=1)
            slope = jnp.dot(slope_t[rows, :], points, preferred_element_type=F32)
            speed = jnp.concatenate([fl[4 * j + i, rows, :] for i in range(4)], axis=1)
            forcing = (-speed.astype(F32) * slope).astype(BF16)
            macc[...] += jnp.dot(fourier_t[:, rows], forcing, preferred_element_type=F32)
            return carry

        lax.fori_loop(0, N_PHI // KB, longitudes, 0)
        for i in range(4):
            done = (macc[:, 128 * i : 128 * i + 128] * (2.0 / N_PHI)).astype(BF16)
            msend[buf, :, i] = done.reshape(PEERS, 16, 128)
        all_to_all(
            lambda dest: msend.at[buf, dest], mrecv.at[j, me], m_send.at[j], m_recv.at[j]
        )

    def arrange(j):
        wait_bytes(mrecv.at[j], m_recv.at[j])

        def unpack(p, carry):
            rows = pl.ds(pl.multiple_of(64 * p, 64), 64)
            for core in range(2):
                wide[core, rows, :] = mrecv[j, 2 * p + core].reshape(64, 128).astype(F32)
            return carry

        lax.fori_loop(0, 16, unpack, 0)

        def one(slot, carry):
            for part in range(2):
                for block in range(0, 8, 2):
                    tiles = [
                        [
                            wide[core, pl.ds(128 * (block + q) + 8 * part + slot, 8, stride=16), :]
                            for core in range(2)
                        ]
                        for q in range(2)
                    ]
                    both = jnp.concatenate(
                        [jnp.concatenate(pieces, axis=1) for pieces in tiles], axis=0
                    )
                    at = 64 * part + 8 * block
                    mx[j, slot, at : at + 16, :] = both.astype(BF16)
            return carry

        lax.fori_loop(0, 8, one, 0)

    def reduce_first(j):
        buf = j % 2
        if j >= 2:
            wait_bytes(r1send.at[buf], r1_ssem.at[j - 2])
            wait_bytes(r2send.at[buf], r2_ssem.at[j - 2])

        def foreign(slot, carry):
            sums = lax.dot_general(
                wt[slot, 256:, :], mx[j, slot], NT, preferred_element_type=F32
            ).astype(BF16)
            r2send[buf, 0, slot] = sums[:256]
            r1send[buf, slot] = sums[256:512]
            r2send[buf, 1, slot] = sums[512:]
            return carry

        lax.fori_loop(0, 8, foreign, 0)
        for half, row in ((0, up), (1, down)):
            span = pl.ds(4 * half, 4)
            remote(
                r1send.at[buf, span], r1recv.at[j, span],
                r1_ssem.at[j], r1_rsem.at[j, half], (2 * row + c, lat),
            )
        reduce_send(j, 0, up, 1)
        reduce_send(j, 1, down, 0)

    def reduce_send(j, way, row, half):
        span = pl.ds(4 * half, 4)
        remote(
            r2send.at[j % 2, way, span], r2recv.at[j, way, span],
            r2_ssem.at[j], r2_rsem.at[j, way, half], (2 * row + c, lat),
        )

    def reduce_second(j):
        for way, row, half in ((0, up, 0), (1, down, 1)):
            span = pl.ds(4 * half, 4)
            wait_bytes(r1recv.at[j, span], r1_rsem.at[j, half])

            def near(slot, carry):
                total = r2send[j % 2, way, slot].astype(F32) + r1recv[j, slot].astype(F32)
                r2send[j % 2, way, slot] = total.astype(BF16)
                return carry

            lax.fori_loop(4 * half, 4 * half + 4, near, 0)
            reduce_send(j, way, row, half)

    def finish(j):
        buf = j % 2
        for way in range(2):
            for half in range(2):
                span = pl.ds(4 * half, 4)
                wait_bytes(r2recv.at[j, way, span], r2_rsem.at[j, way, half])
        lanes = pl.ds(pl.multiple_of(256 * y, 256), 256)
        eye = (
            lax.broadcasted_iota(jnp.int32, (256, 256), 0)
            == lax.broadcasted_iota(jnp.int32, (256, 256), 1)
        ).astype(F32).astype(BF16)

        def one(slot, carry):
            own = ef[j, :, slot, :, lanes].astype(F32)
            own = jnp.concatenate([own[:, :8], own[:, 8:]], axis=0).reshape(128, 256)
            total = lax.dot_general(
                wt[slot, :256, :], mx[j, slot], NT, preferred_element_type=F32
            ) + lax.dot_general(eye, own.astype(BF16), NT, preferred_element_type=F32)
            total += r2recv[j, 0, slot].astype(F32) + r2recv[j, 1, slot].astype(F32)
            for core in range(2):
                for p in range(16):
                    at = 128 * core + 8 * p
                    wide[core, pl.ds(64 * p + slot, 8, stride=8), :] = total[at : at + 8]
            return carry

        lax.fori_loop(0, 8, one, 0)
        if j >= 2:
            sent(fsend.at[buf], f_send.at[j - 2])
            wait_bytes(fr.at[j - 2], f_recv.at[j - 2])

        def pack(p, carry):
            rows = pl.ds(pl.multiple_of(64 * p, 64), 64)
            for core in range(2):
                fsend[buf, 2 * p + core] = wide[core, rows, :].astype(BF16)
            return carry

        lax.fori_loop(0, 16, pack, 0)
        all_to_all(lambda dest: fsend.at[buf, dest], fr.at[j, me], f_send.at[j], f_recv.at[j])

    gather_direct(0)
    mine = pl.ds(pl.multiple_of(128 * c, 128), 128)
    remote(
        leg.at[pl.ds(8 * (1 - c), 8)], lg.at[:, mine, :], lg_send, lg_recv, (2 * y + 1 - c, lat)
    )
    pltpu.make_async_copy(leg.at[pl.ds(8 * c, 8)], lg.at[:, mine, :], lg_recv).start()
    def spread(degree, carry):
        source = lax.broadcasted_iota(jnp.int32, (256, 512), 0)
        lane = lax.broadcasted_iota(jnp.int32, (256, 512), 1)
        level = (lane % 64) // 4 * 16 + lane // 128 * 4 + lane % 4
        hits = (source == level).astype(F32).astype(BF16)
        lg[degree, :, :512] = jnp.dot(inv[degree], hits, preferred_element_type=F32).astype(BF16)
        return carry

    def out_copy(degree):
        return pltpu.make_async_copy(wt.at[degree, pl.ds(0, 512), :], out.at[degree], out_sem)

    def radial(index, carry):
        rows = pl.ds(pl.multiple_of(16 * index, 16), 16)
        part = lax.broadcasted_iota(jnp.int32, (256, 512), 1) % 128 // 64
        piece = fr[:, :, rows, :].astype(F32)
        for u in range(2):
            flat = piece[:, :, 8 * u : 8 * u + 8, :].reshape(CHUNKS, 256, 128)
            left = jnp.concatenate([flat[j] for j in range(CHUNKS)], axis=1)
            degree = 2 * index + u
            for half in range(2):
                wt[degree, 256 * half : 256 * half + 256, :] = lax.dot_general(
                    jnp.where(part == half, left, 0.0).astype(BF16), lg[degree, :, :512], NT,
                    preferred_element_type=F32,
                ).astype(BF16)
            out_copy(degree).start()
        return carry

    gather_direct(1)
    wait_bytes(lg, lg_recv)
    lax.fori_loop(0, 8, mask, 0)
    lax.fori_loop(0, 8, weigh, 0)
    gather_forward(0)
    lax.fori_loop(0, N_PHI // FB, turn_flow, 0)
    gather_forward(1)
    m_row = lax.fori_loop(0, 256, column_order, jnp.zeros((1, 512), F32))
    slope_rows(m_row)
    fourier_rows(m_row)
    synthesize(0)
    gather_direct(2)
    gather_direct(3)
    synthesize(1)
    grid(0)
    gather_forward(2)
    grid(1)
    gather_forward(3)
    arrange(0)
    reduce_first(0)
    synthesize(2)
    synthesize(3)
    arrange(1)
    reduce_first(1)
    reduce_second(0)
    grid(2)
    reduce_second(1)
    grid(3)
    own_inverses.wait()
    lax.fori_loop(0, 8, spread, 0)
    arrange(2)
    reduce_first(2)
    finish(0)
    finish(1)
    reduce_second(2)
    arrange(3)
    reduce_first(3)
    finish(2)
    reduce_second(3)
    finish(3)
    for j in range(CHUNKS):
        wait_bytes(ef.at[j, pl.ds(0, 7)], ag_send.at[j])
    for j in range(CHUNKS - 2, CHUNKS):
        sent(gsend.at[j % 2], g_send.at[j])
        sent(msend.at[j % 2], m_send.at[j])
        wait_bytes(r1send.at[j % 2], r1_ssem.at[j])
        wait_bytes(r2send.at[j % 2], r2_ssem.at[j])
        sent(fsend.at[j % 2], f_send.at[j])
        wait_bytes(fr.at[j], f_recv.at[j])
    wait_bytes(lg.at[:, pl.ds(0, 128), :], lg_send)
    lax.fori_loop(0, 4, radial, 0)
    wait_bytes(wt.at[:, pl.ds(0, 512), :], out_sem)


def shards(entropy, legendre, quad_weights, azimuthal_orders, azimuthal_flow, radial_inverses):
    ent = jnp.transpose(entropy, (0, 2, 3, 1)).reshape(16, 64, N_DEG)
    hbm = pl.BlockSpec(memory_space=pl.ANY)
    vmem = pl.BlockSpec(memory_space=pltpu.VMEM)
    smem = pl.BlockSpec(memory_space=pltpu.SMEM)
    dma = pltpu.SemaphoreType.DMA
    updated = pl.pallas_call(
        kernel,
        out_shape=jax.ShapeDtypeStruct((8, 512, 256), BF16),
        in_specs=[hbm, hbm, vmem, smem, hbm, hbm],
        out_specs=hbm,
        scratch_shapes=[
            pltpu.VMEM((16, 64, N_DEG), BF16),
            pltpu.VMEM((8, 256, 256), BF16),
            pltpu.VMEM((CHUNKS, PEERS, 64, 128), BF16),
            pltpu.VMEM((CHUNKS, 8, 8, 16, N_DEG), BF16),
            pltpu.VMEM((8, 256, N_DEG), BF16),
            pltpu.VMEM((8, N_DEG, 256), BF16),
            pltpu.VMEM((N_PHI, 512), BF16),
            pltpu.VMEM((512, N_PHI), BF16),
            pltpu.VMEM((16, N_PHI, 128), BF16),
            pltpu.VMEM((2, FB, 16, 128), BF16),
            pltpu.VMEM((2, 64, 512), F32),
            pltpu.VMEM((2, PEERS, 4, 16, 128), BF16),
            pltpu.VMEM((CHUNKS, 4, 512, 128), BF16),
            pltpu.VMEM((2, PEERS, 4, 16, 128), BF16),
            pltpu.VMEM((CHUNKS, PEERS, 4, 16, 128), BF16),
            pltpu.VMEM((CHUNKS, 8, 128, 256), BF16),
            pltpu.VMEM((2, 1024, 128), F32),
            pltpu.VMEM((512, 512), F32),
            pltpu.VMEM((2, 8, 256, 128), BF16),
            pltpu.VMEM((CHUNKS, 8, 256, 128), BF16),
            pltpu.VMEM((2, 2, 8, 256, 128), BF16),
            pltpu.VMEM((CHUNKS, 2, 8, 256, 128), BF16),
            pltpu.VMEM((2, PEERS, 64, 128), BF16),
            dma((CHUNKS,)), dma((CHUNKS, 8)), dma, dma, dma((2,)),
            dma((CHUNKS,)), dma((CHUNKS,)), dma((CHUNKS,)), dma((CHUNKS,)),
            dma((CHUNKS,)), dma((CHUNKS, 2)), dma((CHUNKS,)), dma((CHUNKS, 2, 2)),
            dma((CHUNKS,)), dma((CHUNKS,)), dma, dma, dma,
        ],
        compiler_params=pltpu.CompilerParams(
            collective_id=0, has_side_effects=True, vmem_limit_bytes=62 * 1024 * 1024
        ),
        cost_estimate=pl.CostEstimate(
            flops=17_000_000_000, bytes_accessed=24_000_000, transcendentals=0
        ),
    )(
        ent, legendre, quad_weights.reshape(8, 128), azimuthal_orders, azimuthal_flow,
        radial_inverses,
    )
    return jnp.transpose(updated.reshape(8, 2, 256, 256), (2, 0, 1, 3))


def solution(mesh):
    placed = (
        P("lat", None, None, "rad"),
        P("lat", "rad", None),
        P(),
        P(),
        P(None, "lat", "rad"),
        P(("rad", "lat"), None, None),
    )
    return jax.shard_map(
        shards,
        mesh=mesh,
        in_specs=placed,
        out_specs=P(None, ("rad", "lat"), None, None),
        check_vma=False,
    )
```

```python
import math

import jax
import jax.numpy as jnp
from jax import lax
from jax.experimental import pallas as pl
from jax.experimental.pallas import tpu as pltpu
from jax.sharding import PartitionSpec as P

MESH = pl.DeviceIdType.MESH
F32, BF16 = jnp.float32, jnp.bfloat16
N_DEG = 1024
N_PHI = 3072
PEERS = 32
CHUNKS = 4
NT = (((1,), (1,)), ((), ()))
KB = 512
FB = 128
ORDER = (
    "D0", "X", "D1", "M", "F0", "T", "F1", "P", "S0", "D2", "D3", "S1", "G0", "F2", "G1", "F3",
    "A0", "S2", "S3", "A1", "B0", "G2", "B1", "G3", "V", "A2", "Y0", "Z0", "Y1", "Z1", "B2", "A3",
    "Y2", "Z2", "B3", "E", "Y3", "Z3",
)


def halves(values):
    high = values.astype(BF16)
    return high, (values - high.astype(F32)).astype(BF16)


def wait_bytes(ref, sem):
    pltpu.make_async_copy(ref, ref, sem).wait()


def waves(product):
    turns = jnp.floor(product * (4.0 / N_PHI) + 0.5)
    x = (product - turns * (N_PHI // 4)) * (2.0 * math.pi / N_PHI)
    x2 = x * x
    sine = x * (1.0 + x2 * (-1 / 6 + x2 * (1 / 120 + x2 * (-1 / 5040 + x2 * (1 / 362880)))))
    cosine = 1.0 + x2 * (-0.5 + x2 * (1 / 24 + x2 * (-1 / 720 + x2 * (1 / 40320))))
    quarter = turns - 4.0 * jnp.floor(turns * 0.25)
    odd = (quarter == 1.0) | (quarter == 3.0)
    first = jnp.where(odd, sine, cosine)
    second = jnp.where(odd, cosine, sine)
    cos = jnp.where((quarter == 1.0) | (quarter == 2.0), -first, first)
    sin = jnp.where(quarter >= 2.0, -second, second)
    return cos, sin


def kernel(
    ent, leg, qw, orders, order_lanes, flow, inverses, out,
    er, inv, fr, ef, lg, wt, slope_t, fourier_t, fl, tb, gsend, grecv, msend, mrecv, mx, pre, wide, macc,
    r1send, r1recv, r2send, r2recv, fsend,
    ag_send, ag_recv, lg_send, lg_recv, raw_sem, g_send, g_recv, m_send, m_recv,
    r1_ssem, r1_rsem, r2_ssem, r2_rsem, f_send, f_recv, er_sem, inv_sem, out_sem,
):
    rad = lax.axis_index("rad")
    lat = lax.axis_index("lat")
    y, c = rad // 2, rad % 2
    me = 2 * lat + c
    up, down, across = (y + 1) % 4, (y + 3) % 4, (y + 2) % 4

    def place(index):
        return (2 * y + index % 2, index // 2)

    def raw_copy(block):
        pieces = flow.at[pl.ds(FB // 16 * block, FB // 16)]
        place = r2send.at[block % 4 // 2, block % 2]
        return pltpu.make_async_copy(pieces, place, raw_sem.at[block % 4])

    own_rows = pltpu.make_async_copy(ent, er, er_sem)
    own_rows.start()
    for block in range(4):
        raw_copy(block).start()
    own_inverses = pltpu.make_async_copy(inverses, inv, inv_sem)
    own_inverses.start()

    barrier = pltpu.get_barrier_semaphore()

    def greet(offset, carry):
        pl.semaphore_signal(
            barrier, inc=1, device_id=place((me + offset) % PEERS), device_id_type=MESH
        )
        return carry

    lax.fori_loop(1, PEERS, greet, 0)
    for row in (up, down):
        for core in range(2):
            pl.semaphore_signal(
                barrier, inc=1, device_id=(2 * row + core, lat), device_id_type=MESH
            )

    def regroup(slot, carry):
        rows = er[slot].astype(F32).reshape(4, 16, N_DEG)
        low = lax.broadcasted_iota(jnp.int32, (8, N_DEG), 0) < 4
        for j in range(CHUNKS):
            tiles = []
            for part in range(2):
                first = rows[2 * part, 8 * (j // 2) : 8 * (j // 2) + 8]
                second = rows[2 * part + 1, 8 * (j // 2) : 8 * (j // 2) + 8]
                if j % 2 == 0:
                    tiles.append(jnp.where(low, first, pltpu.roll(second, 4, axis=0)))
                else:
                    tiles.append(jnp.where(low, pltpu.roll(first, 4, axis=0), second))
            er[slot, 16 * j : 16 * j + 16, :] = jnp.concatenate(tiles, axis=0).astype(BF16)
        return carry

    own_rows.wait()
    lax.fori_loop(0, 16, regroup, 0)
    pl.semaphore_wait(barrier, PEERS - 1 + 4)

    def remote(src, dst, send_sem, recv_sem, device):
        pltpu.make_async_remote_copy(
            src_ref=src, dst_ref=dst, send_sem=send_sem, recv_sem=recv_sem,
            device_id=device, device_id_type=MESH,
        ).start()

    def all_to_all(source, target, send_sem, recv_sem):
        pltpu.make_async_copy(source(me), target, recv_sem).start()

        def send(offset, carry):
            dest = (me + offset) % PEERS
            remote(source(dest), target, send_sem, recv_sem, place(dest))
            return carry

        lax.fori_loop(1, PEERS, send, 0)

    def sent(buffer, sem):
        wait_bytes(buffer.at[pl.ds(0, PEERS - 1)], sem)

    def gather_direct(j):
        rows = pl.ds(16 * j, 16)
        for row in (up, down):
            for core in range(2):
                remote(
                    er.at[pl.ds(8 * core, 8), rows, :], ef.at[j, rad],
                    ag_send.at[j], ag_recv.at[j, rad], (2 * row + core, lat),
                )
        remote(
            er.at[pl.ds(8 * (1 - c), 8), rows, :], ef.at[j, rad],
            ag_send.at[j], ag_recv.at[j, rad], (2 * y + 1 - c, lat),
        )
        pltpu.make_async_copy(
            er.at[pl.ds(8 * c, 8), rows, :], ef.at[j, rad], ag_recv.at[j, rad]
        ).start()

    def gather_wait(j, block):
        wait_bytes(ef.at[j, block], ag_recv.at[j, block])

    def gather_forward(j):
        for block, row in ((2 * down, up), (2 * up + 1, down)):
            gather_wait(j, block)
            remote(
                ef.at[j, block], ef.at[j, block],
                ag_send.at[j], ag_recv.at[j, block], (2 * row + c, lat),
            )

    def gather_rest(j):
        for block in (rad, 2 * y + 1 - c, 2 * down + 1, 2 * up, 2 * across, 2 * across + 1):
            gather_wait(j, block)

    columns = lax.broadcasted_iota(jnp.int32, (1, 512), 1)

    def order_row():
        wide_columns = lax.broadcasted_iota(jnp.int32, (256, 512), 1)
        slots = wide_columns // 16 * 8 + wide_columns % 8
        hits = (lax.broadcasted_iota(jnp.int32, (256, 512), 0) == slots).astype(F32).astype(BF16)
        held = jnp.concatenate([order_lanes[0:1, :], order_lanes[1:2, :]], axis=1).astype(F32)
        held = jnp.broadcast_to(held, (8, 256))
        high = jnp.floor(held * (1 / 32))
        low = held - 32.0 * high
        row = 32.0 * jnp.dot(high.astype(BF16), hits, preferred_element_type=F32)
        return (row + jnp.dot(low.astype(BF16), hits, preferred_element_type=F32))[0:1, :]

    def slope_rows(m_row):
        quarter = jnp.where(columns % 16 >= 8, N_PHI / 4, 0.0)
        cos_b, sin_b = waves(lax.broadcasted_iota(jnp.int32, (64, 512), 0).astype(F32) * m_row)
        tb[0] = cos_b
        tb[1] = sin_b
        scaled = m_row * (1.0 / N_DEG)

        def rows(a, carry):
            cos_a, sin_a = waves((64 * a).astype(F32) * m_row + quarter)
            sines = sin_a * tb[0] + cos_a * tb[1]
            slope_t[pl.ds(pl.multiple_of(64 * a, 64), 64), :] = (-(scaled * sines)).astype(BF16)
            return carry

        lax.fori_loop(0, N_PHI // 64, rows, 0)

    def fourier_rows(m_row):
        macc[:, :128] = jnp.transpose(jnp.broadcast_to(m_row, (128, 512)))
        lanes = lax.broadcasted_iota(jnp.int32, (64, 128), 1).astype(F32)
        second = lax.broadcasted_iota(jnp.int32, (64, 128), 0) % 16 >= 8
        quarter = jnp.where(second, N_PHI / 4, 0.0)

        def rows_of(block, carry):
            rows = pl.ds(pl.multiple_of(64 * block, 64), 64)
            m = macc[rows, :128]
            cos_b, sin_b = waves(lanes * m)
            cos_a, sin_a = waves(jnp.minimum(lanes, N_PHI // 128 - 1) * 128.0 * m + quarter)
            for a in range(N_PHI // 128):
                cosines = cos_a[:, a : a + 1] * cos_b - sin_a[:, a : a + 1] * sin_b
                fourier_t[rows, 128 * a : 128 * a + 128] = cosines.astype(BF16)
            return carry

        lax.fori_loop(0, 8, rows_of, 0)

    def turn_flow(block, carry):
        raw_copy(block).wait()
        piece = r2send[block % 4 // 2, block % 2].reshape(2, 1024, 128)
        for half in range(2):
            wide[half] = piece[half].astype(F32)

        @pl.when(block + 4 < N_PHI // FB)
        def _():
            raw_copy(block + 4).start()

        for half in range(2):
            rows = pl.ds(pl.multiple_of(FB * block + 64 * half, 64), 64)
            for level in range(16):
                fl[level, rows, :] = wide[half, pl.ds(level, 64, stride=16), :].astype(BF16)
        return carry

    def prepare(slot, carry):
        order = orders[16 * lat + 8 * c + slot]
        weights = jnp.concatenate([qw[pl.ds(2 * y, 1), :], qw[pl.ds(2 * y + 1, 1), :]], axis=1)
        for quarter in range(4):
            block = jnp.transpose(lg[slot, :, 256 * quarter : 256 * quarter + 256].astype(F32))
            degrees = lax.broadcasted_iota(jnp.int32, block.shape, 0) + 256 * quarter
            block = jnp.where(degrees >= order, block, 0.0)
            lg[slot, :, 256 * quarter : 256 * quarter + 256] = block.astype(BF16)
            rows = pl.ds(pl.multiple_of(256 * ((quarter - y + 4) % 4), 256), 256)
            wt[slot, rows, :] = (block * weights).astype(BF16)
        return carry

    def synthesize(j):
        gather_rest(j)
        lanes = pl.ds(pl.multiple_of(256 * y, 256), 256)
        eye = (
            lax.broadcasted_iota(jnp.int32, (256, 256), 0)
            == lax.broadcasted_iota(jnp.int32, (256, 256), 1)
        ).astype(F32).astype(BF16)

        def one(slot, carry):
            values = jnp.zeros((128, 256), F32)
            for quarter in range(4):
                span = pl.ds(256 * quarter, 256)
                values += jnp.dot(
                    ef[j, :, slot, :, span].reshape(128, 256), lg[slot, :, span],
                    preferred_element_type=F32,
                )
            own = ef[j, :, slot, :, lanes].astype(F32)
            own = jnp.concatenate([own[:, :8], own[:, 8:]], axis=0).reshape(128, 256)
            pre[j, slot] = lax.dot_general(
                eye, own.astype(BF16), NT, preferred_element_type=F32
            ).astype(BF16)
            for block in range(8):
                for part in range(2):
                    at = 16 * block + 8 * part
                    for core in range(2):
                        wide[core, pl.ds(128 * block + 8 * part + slot, 8, stride=16), :] = values[
                            at : at + 8, 128 * core : 128 * core + 128
                        ]
            return carry

        lax.fori_loop(0, 8, one, 0)
        buf = j % 2
        if j >= 2:
            sent(gsend.at[buf], g_send.at[j - 2])

        def pack(p, carry):
            rows = pl.ds(pl.multiple_of(64 * p, 64), 64)
            for core in range(2):
                gsend[buf, 2 * p + core] = wide[core, rows, :].astype(BF16).reshape(4, 16, 128)
            return carry

        lax.fori_loop(0, 16, pack, 0)
        all_to_all(
            lambda dest: gsend.at[buf, dest], grecv.at[j, :, pl.ds(16 * me, 16), :],
            g_send.at[j], g_recv.at[j],
        )

    def grid(j):
        wait_bytes(grecv.at[j], g_recv.at[j])
        buf = j % 2
        if j >= 2:
            sent(msend.at[buf], m_send.at[j - 2])

        macc[...] = jnp.zeros_like(macc)

        def longitudes(kb, carry):
            rows = pl.ds(pl.multiple_of(KB * kb, KB), KB)
            points = jnp.concatenate([grecv[j, i] for i in range(4)], axis=1)
            slope = jnp.dot(slope_t[rows, :], points, preferred_element_type=F32)
            speed = jnp.concatenate([fl[4 * j + i, rows, :] for i in range(4)], axis=1)
            forcing = (-speed.astype(F32) * slope).astype(BF16)
            macc[...] += jnp.dot(fourier_t[:, rows], forcing, preferred_element_type=F32)
            return carry

        lax.fori_loop(0, N_PHI // KB, longitudes, 0)
        for i in range(4):
            done = (macc[:, 128 * i : 128 * i + 128] * (2.0 / N_PHI)).astype(BF16)
            msend[buf, :, i] = done.reshape(PEERS, 16, 128)
        all_to_all(
            lambda dest: msend.at[buf, dest], mrecv.at[j, me], m_send.at[j], m_recv.at[j]
        )

    def arrange(j):
        wait_bytes(mrecv.at[j], m_recv.at[j])

        def unpack(p, carry):
            rows = pl.ds(pl.multiple_of(64 * p, 64), 64)
            for core in range(2):
                wide[core, rows, :] = mrecv[j, 2 * p + core].reshape(64, 128).astype(F32)
            return carry

        lax.fori_loop(0, 16, unpack, 0)

        def one(slot, carry):
            for part in range(2):
                for block in range(0, 8, 2):
                    tiles = [
                        [
                            wide[core, pl.ds(128 * (block + q) + 8 * part + slot, 8, stride=16), :]
                            for core in range(2)
                        ]
                        for q in range(2)
                    ]
                    both = jnp.concatenate(
                        [jnp.concatenate(pieces, axis=1) for pieces in tiles], axis=0
                    )
                    at = 64 * part + 8 * block
                    mx[slot, at : at + 16, :] = both.astype(BF16)
            return carry

        lax.fori_loop(0, 8, one, 0)

    def reduce_first(j):
        buf = j % 2
        if j >= 2:
            wait_bytes(r1send.at[buf], r1_ssem.at[j - 2])
            wait_bytes(r2send.at[buf], r2_ssem.at[j - 2])

        def foreign(slot, carry):
            sums = lax.dot_general(wt[slot], mx[slot], NT, preferred_element_type=F32)
            rows = pl.ds(pl.multiple_of(256 * slot, 256), 256)
            own = sums[:256] + pre[j, slot].astype(F32)
            pre[j, slot], fl[4 * j, rows, :] = halves(own)
            r2send[buf, 0, slot], fl[4 * j + 1, rows, :] = halves(sums[256:512])
            r1send[buf, slot] = sums[512:768].astype(BF16)
            r2send[buf, 1, slot], fl[4 * j + 2, rows, :] = halves(sums[768:])
            return carry

        lax.fori_loop(0, 8, foreign, 0)
        for half, row in ((0, up), (1, down)):
            span = pl.ds(4 * half, 4)
            remote(
                r1send.at[buf, span], r1recv.at[j, span],
                r1_ssem.at[j], r1_rsem.at[j, half], (2 * row + c, lat),
            )
        for part in range(2):
            reduce_send(j, 0, up, 1, part)
            reduce_send(j, 1, down, 0, part)

    def reduce_send(j, way, row, half, part):
        span, rows = pl.ds(4 * half, 4), pl.ds(128 * part, 128)
        remote(
            r2send.at[j % 2, way, span, rows, :], r2recv.at[j, way, span, rows, :],
            r2_ssem.at[j], r2_rsem.at[j, way, half, part], (2 * row + c, lat),
        )

    def reduce_second(j):
        for half in range(2):
            wait_bytes(r1recv.at[j, pl.ds(4 * half, 4)], r1_rsem.at[j, half])
        for part in range(2):
            rows = pl.ds(128 * part, 128)
            for way, row, half in ((0, up, 0), (1, down, 1)):

                def near(slot, carry):
                    lows = pl.ds(pl.multiple_of(256 * slot + 128 * part, 128), 128)
                    total = r2send[j % 2, way, slot, rows, :].astype(F32)
                    total += fl[4 * j + 1 + way, lows, :].astype(F32)
                    total += r1recv[j, slot, rows, :].astype(F32)
                    r2send[j % 2, way, slot, rows, :] = total.astype(BF16)
                    return carry

                lax.fori_loop(4 * half, 4 * half + 4, near, 0)
                reduce_send(j, way, row, half, part)

    def finish(j, part):
        buf = j % 2
        rows = pl.ds(128 * part, 128)
        for way in range(2):
            for half in range(2):
                span = pl.ds(4 * half, 4)
                wait_bytes(r2recv.at[j, way, span, rows, :], r2_rsem.at[j, way, half, part])

        def one(slot, carry):
            lows = pl.ds(pl.multiple_of(256 * slot + 128 * part, 128), 128)
            total = pre[j, slot, rows, :].astype(F32) + fl[4 * j, lows, :].astype(F32)
            total += r2recv[j, 0, slot, rows, :].astype(F32)
            total += r2recv[j, 1, slot, rows, :].astype(F32)
            for p in range(16):
                wide[part, pl.ds(64 * p + slot, 8, stride=8), :] = total[8 * p : 8 * p + 8]
            return carry

        lax.fori_loop(0, 8, one, 0)
        if j >= 2 and part == 0:
            sent(fsend.at[buf], f_send.at[j - 2])
            if j == 2:
                wait_bytes(fr.at[0], f_recv.at[0])

        def pack(p, carry):
            span = pl.ds(pl.multiple_of(64 * p, 64), 64)
            fsend[buf, 2 * p + part] = wide[part, span, :].astype(BF16)
            return carry

        lax.fori_loop(0, 16, pack, 0)

        def send(offset, carry):
            p = (lat + offset) % 16
            remote(
                fsend.at[buf, 2 * p + part], fr.at[j, me],
                f_send.at[j], f_recv.at[j], (2 * y + part, p),
            )
            return carry

        lax.fori_loop(1, 16, send, 0)

        @pl.when(c == part)
        def _():
            pltpu.make_async_copy(fsend.at[buf, me], fr.at[j, me], f_recv.at[j]).start()

        @pl.when(c != part)
        def _():
            remote(
                fsend.at[buf, 2 * lat + part], fr.at[j, me],
                f_send.at[j], f_recv.at[j], (2 * y + part, lat),
            )

    def spread(degree, carry):
        source = lax.broadcasted_iota(jnp.int32, (256, 512), 0)
        lane = lax.broadcasted_iota(jnp.int32, (256, 512), 1)
        level = (lane % 64) // 4 * 16 + lane // 128 * 4 + lane % 4
        hits = (source == level).astype(F32).astype(BF16)
        lg[degree, :, :512] = jnp.dot(inv[degree], hits, preferred_element_type=F32).astype(BF16)
        return carry

    def out_copy(degree):
        return pltpu.make_async_copy(wt.at[degree, pl.ds(0, 512), :], out.at[degree], out_sem)

    def update(chunks, degree_pair, store):
        rows = pl.ds(pl.multiple_of(16 * degree_pair, 16), 16)
        width = 128 * len(chunks)
        part = lax.broadcasted_iota(jnp.int32, (256, width), 1) % 128 // 64
        pieces = [fr[j, :, rows, :].astype(F32) for j in chunks]
        for u in range(2):
            flat = [piece[:, 8 * u : 8 * u + 8, :].reshape(256, 128) for piece in pieces]
            left = jnp.concatenate(flat, axis=1)
            degree = 2 * degree_pair + u
            for half in range(2):
                right = lg[degree, :, 128 * chunks[0] : 128 * chunks[0] + width]
                store(degree, half, lax.dot_general(
                    jnp.where(part == half, left, 0.0).astype(BF16), right, NT,
                    preferred_element_type=F32,
                ))

    def early(degree_pair, carry):
        def store(degree, half, values):
            rows = pl.ds(pl.multiple_of(256 * degree, 256), 256)
            span = pl.ds(256 * half, 256)
            lg[degree, :, pl.ds(512 + 256 * half, 256)], slope_t[rows, span] = halves(values)

        update((0, 1, 2), degree_pair, store)
        return carry

    def late(degree_pair, carry):
        def store(degree, half, values):
            rows = pl.ds(pl.multiple_of(256 * degree, 256), 256)
            values += lg[degree, :, 512 + 256 * half : 768 + 256 * half].astype(F32)
            values += slope_t[rows, 256 * half : 256 * half + 256].astype(F32)
            wt[degree, 256 * half : 256 * half + 256, :] = values.astype(BF16)

        update((3,), degree_pair, store)
        for u in range(2):
            out_copy(2 * degree_pair + u).start()
        return carry

    def prepare_legendre():
        wait_bytes(lg, lg_recv)
        lax.fori_loop(0, 8, prepare, 0)

    def prepare_flow():
        lax.fori_loop(0, N_PHI // FB, turn_flow, 0)

    def prepare_tables():
        m_row = order_row()
        slope_rows(m_row)
        fourier_rows(m_row)

    def prepare_inverses():
        own_inverses.wait()
        lax.fori_loop(0, 8, spread, 0)

    def begin_radial():
        for j in (1, 2):
            wait_bytes(fr.at[j], f_recv.at[j])
        lax.fori_loop(0, 4, early, 0)

    def swap_tables():
        mine = pl.ds(pl.multiple_of(128 * c, 128), 128)
        remote(
            leg.at[pl.ds(8 * (1 - c), 8)], lg.at[:, mine, :], lg_send, lg_recv,
            (2 * y + 1 - c, lat),
        )
        pltpu.make_async_copy(leg.at[pl.ds(8 * c, 8)], lg.at[:, mine, :], lg_recv).start()

    steps = dict(
        D=gather_direct, F=gather_forward, S=synthesize, G=grid, B=reduce_second,
        X=swap_tables, M=prepare_legendre, T=prepare_flow, P=prepare_tables,
        V=prepare_inverses, E=begin_radial, Y=lambda j: finish(j, 0), Z=lambda j: finish(j, 1),
    )
    for step in ORDER:
        if step[0] == "A":
            arrange(int(step[1]))
            reduce_first(int(step[1]))
        else:
            steps[step[0]](*(int(digit) for digit in step[1:]))

    for j in range(CHUNKS):
        wait_bytes(ef.at[j, pl.ds(0, 7)], ag_send.at[j])
    wait_bytes(lg.at[:, pl.ds(0, 128), :], lg_send)
    for j in range(CHUNKS - 2, CHUNKS):
        sent(gsend.at[j % 2], g_send.at[j])
        sent(msend.at[j % 2], m_send.at[j])
        wait_bytes(r1send.at[j % 2], r1_ssem.at[j])
        wait_bytes(r2send.at[j % 2], r2_ssem.at[j])
        sent(fsend.at[j % 2], f_send.at[j])
    wait_bytes(fr.at[3], f_recv.at[3])
    lax.fori_loop(0, 4, late, 0)
    wait_bytes(wt.at[:, pl.ds(0, 512), :], out_sem)


def shards(entropy, legendre, quad_weights, azimuthal_orders, azimuthal_flow, radial_inverses):
    ent = jnp.transpose(entropy, (0, 2, 3, 1)).reshape(16, 64, N_DEG)
    hbm = pl.BlockSpec(memory_space=pl.ANY)
    vmem = pl.BlockSpec(memory_space=pltpu.VMEM)
    smem = pl.BlockSpec(memory_space=pltpu.SMEM)
    dma = pltpu.SemaphoreType.DMA
    updated = pl.pallas_call(
        kernel,
        out_shape=jax.ShapeDtypeStruct((8, 512, 256), BF16),
        in_specs=[hbm, hbm, vmem, smem, vmem, hbm, hbm],
        out_specs=hbm,
        scratch_shapes=[
            pltpu.VMEM((16, 64, N_DEG), BF16),
            pltpu.VMEM((8, 256, 256), BF16),
            pltpu.VMEM((CHUNKS, PEERS, 64, 128), BF16),
            pltpu.VMEM((CHUNKS, 8, 8, 16, N_DEG), BF16),
            pltpu.VMEM((8, 256, N_DEG), BF16),
            pltpu.VMEM((8, N_DEG, 256), BF16),
            pltpu.VMEM((N_PHI, 512), BF16),
            pltpu.VMEM((512, N_PHI), BF16),
            pltpu.VMEM((16, N_PHI, 128), BF16),
            pltpu.VMEM((2, 64, 512), F32),
            pltpu.VMEM((2, PEERS, 4, 16, 128), BF16),
            pltpu.VMEM((CHUNKS, 4, 512, 128), BF16),
            pltpu.VMEM((2, PEERS, 4, 16, 128), BF16),
            pltpu.VMEM((CHUNKS, PEERS, 4, 16, 128), BF16),
            pltpu.VMEM((8, 128, 256), BF16),
            pltpu.VMEM((CHUNKS, 8, 256, 128), BF16),
            pltpu.VMEM((2, 1024, 128), F32),
            pltpu.VMEM((512, 512), F32),
            pltpu.VMEM((2, 8, 256, 128), BF16),
            pltpu.VMEM((CHUNKS, 8, 256, 128), BF16),
            pltpu.VMEM((2, 2, 8, 256, 128), BF16),
            pltpu.VMEM((CHUNKS, 2, 8, 256, 128), BF16),
            pltpu.VMEM((2, PEERS, 64, 128), BF16),
            dma((CHUNKS,)), dma((CHUNKS, 8)), dma, dma, dma((4,)),
            dma((CHUNKS,)), dma((CHUNKS,)), dma((CHUNKS,)), dma((CHUNKS,)),
            dma((CHUNKS,)), dma((CHUNKS, 2)), dma((CHUNKS,)), dma((CHUNKS, 2, 2, 2)),
            dma((CHUNKS,)), dma((CHUNKS,)), dma, dma, dma,
        ],
        compiler_params=pltpu.CompilerParams(
            collective_id=0, has_side_effects=True, vmem_limit_bytes=62 * 1024 * 1024
        ),
        cost_estimate=pl.CostEstimate(
            flops=17_000_000_000, bytes_accessed=24_000_000, transcendentals=0
        ),
    )(
        ent, legendre, quad_weights.reshape(8, 128), azimuthal_orders,
        azimuthal_orders.reshape(2, 128), azimuthal_flow.reshape(N_PHI // 16, 256, 128),
        radial_inverses,
    )
    return jnp.transpose(updated.reshape(8, 2, 256, 256), (2, 0, 1, 3))


def solution(mesh):
    placed = (
        P("lat", None, None, "rad"),
        P("lat", "rad", None),
        P(),
        P(),
        P(None, "lat", "rad"),
        P(("rad", "lat"), None, None),
    )
    return jax.shard_map(
        shards,
        mesh=mesh,
        in_specs=placed,
        out_specs=P(None, ("rad", "lat"), None, None),
        check_vma=False,
    )
```

```python
import math

import jax
import jax.numpy as jnp
from jax import lax
from jax.experimental import pallas as pl
from jax.experimental.pallas import tpu as pltpu
from jax.sharding import PartitionSpec as P

MESH = pl.DeviceIdType.MESH
F32, BF16 = jnp.float32, jnp.bfloat16
N_DEG = 1024
N_PHI = 3072
PEERS = 32
CHUNKS = 4
NT = (((1,), (1,)), ((), ()))
KB = 512
FB = 128
PARTS = 4
ROWS = 256 // PARTS
ORDER = (
    "D0", "X", "D1", "M", "F0", "T", "F1", "P", "S0", "D2", "D3", "S1", "G0", "F2", "G1", "F3",
    "A0", "S2", "S3", "A1", "B0", "G2", "B1", "G3", "V", "A2", "Z00", "Z01", "Z02", "Z03", "Z10",
    "Z11", "Z12", "Z13", "B2", "A3", "Z20", "Z21", "Z22", "Z23", "B3", "Z30", "Z31", "Z32", "Z33", "E",
)


def halves(values):
    high = values.astype(BF16)
    return high, (values - high.astype(F32)).astype(BF16)


def wait_bytes(ref, sem):
    pltpu.make_async_copy(ref, ref, sem).wait()


def waves(product):
    turns = jnp.floor(product * (4.0 / N_PHI) + 0.5)
    x = (product - turns * (N_PHI // 4)) * (2.0 * math.pi / N_PHI)
    x2 = x * x
    sine = x * (1.0 + x2 * (-1 / 6 + x2 * (1 / 120 + x2 * (-1 / 5040 + x2 * (1 / 362880)))))
    cosine = 1.0 + x2 * (-0.5 + x2 * (1 / 24 + x2 * (-1 / 720 + x2 * (1 / 40320))))
    quarter = turns - 4.0 * jnp.floor(turns * 0.25)
    odd = (quarter == 1.0) | (quarter == 3.0)
    first = jnp.where(odd, sine, cosine)
    second = jnp.where(odd, cosine, sine)
    cos = jnp.where((quarter == 1.0) | (quarter == 2.0), -first, first)
    sin = jnp.where(quarter >= 2.0, -second, second)
    return cos, sin


def kernel(
    ent, leg, qw, orders, order_lanes, flow, inverses, out,
    er, inv, fr, ef, lg, wt, slope_t, fourier_t, fl, tb, gsend, grecv, msend, mrecv, mx, pre, wide, macc,
    r1send, r1recv, r2send, r2recv, fsend,
    ag_send, ag_recv, lg_send, lg_recv, raw_sem, g_send, g_recv, m_send, m_recv,
    r1_ssem, r1_rsem, r2_ssem, r2_rsem, f_send, f_recv, er_sem, inv_sem, out_sem,
):
    rad = lax.axis_index("rad")
    lat = lax.axis_index("lat")
    y, c = rad // 2, rad % 2
    me = 2 * lat + c
    up, down, across = (y + 1) % 4, (y + 3) % 4, (y + 2) % 4

    def place(index):
        return (2 * y + index % 2, index // 2)

    def raw_copy(block):
        pieces = flow.at[pl.ds(FB // 16 * block, FB // 16)]
        place = r2send.at[block % 4 // 2, block % 2]
        return pltpu.make_async_copy(pieces, place, raw_sem.at[block % 4])

    own_rows = pltpu.make_async_copy(ent, er, er_sem)
    own_rows.start()
    for block in range(4):
        raw_copy(block).start()
    own_inverses = pltpu.make_async_copy(inverses, inv, inv_sem)
    own_inverses.start()

    barrier = pltpu.get_barrier_semaphore()

    def greet(offset, carry):
        pl.semaphore_signal(
            barrier, inc=1, device_id=place((me + offset) % PEERS), device_id_type=MESH
        )
        return carry

    lax.fori_loop(1, PEERS, greet, 0)
    for row in (up, down):
        for core in range(2):
            pl.semaphore_signal(
                barrier, inc=1, device_id=(2 * row + core, lat), device_id_type=MESH
            )

    def regroup(slot, carry):
        rows = er[slot].astype(F32).reshape(4, 16, N_DEG)
        low = lax.broadcasted_iota(jnp.int32, (8, N_DEG), 0) < 4
        for j in range(CHUNKS):
            tiles = []
            for part in range(2):
                first = rows[2 * part, 8 * (j // 2) : 8 * (j // 2) + 8]
                second = rows[2 * part + 1, 8 * (j // 2) : 8 * (j // 2) + 8]
                if j % 2 == 0:
                    tiles.append(jnp.where(low, first, pltpu.roll(second, 4, axis=0)))
                else:
                    tiles.append(jnp.where(low, pltpu.roll(first, 4, axis=0), second))
            er[slot, 16 * j : 16 * j + 16, :] = jnp.concatenate(tiles, axis=0).astype(BF16)
        return carry

    own_rows.wait()
    lax.fori_loop(0, 16, regroup, 0)
    pl.semaphore_wait(barrier, PEERS - 1 + 4)

    def remote(src, dst, send_sem, recv_sem, device):
        pltpu.make_async_remote_copy(
            src_ref=src, dst_ref=dst, send_sem=send_sem, recv_sem=recv_sem,
            device_id=device, device_id_type=MESH,
        ).start()

    def all_to_all(source, target, send_sem, recv_sem):
        pltpu.make_async_copy(source(me), target, recv_sem).start()

        def send(offset, carry):
            dest = (me + offset) % PEERS
            remote(source(dest), target, send_sem, recv_sem, place(dest))
            return carry

        lax.fori_loop(1, PEERS, send, 0)

    def sent(buffer, sem):
        wait_bytes(buffer.at[pl.ds(0, PEERS - 1)], sem)

    def gather_direct(j):
        rows = pl.ds(16 * j, 16)
        for row in (up, down):
            for core in range(2):
                remote(
                    er.at[pl.ds(8 * core, 8), rows, :], ef.at[j, rad],
                    ag_send.at[j], ag_recv.at[j, rad], (2 * row + core, lat),
                )
        remote(
            er.at[pl.ds(8 * (1 - c), 8), rows, :], ef.at[j, rad],
            ag_send.at[j], ag_recv.at[j, rad], (2 * y + 1 - c, lat),
        )
        pltpu.make_async_copy(
            er.at[pl.ds(8 * c, 8), rows, :], ef.at[j, rad], ag_recv.at[j, rad]
        ).start()

    def gather_wait(j, block):
        wait_bytes(ef.at[j, block], ag_recv.at[j, block])

    def gather_forward(j):
        for block, row in ((2 * down, up), (2 * up + 1, down)):
            gather_wait(j, block)
            remote(
                ef.at[j, block], ef.at[j, block],
                ag_send.at[j], ag_recv.at[j, block], (2 * row + c, lat),
            )

    def gather_rest(j):
        for block in (rad, 2 * y + 1 - c, 2 * down + 1, 2 * up, 2 * across, 2 * across + 1):
            gather_wait(j, block)

    columns = lax.broadcasted_iota(jnp.int32, (1, 512), 1)

    def order_row():
        wide_columns = lax.broadcasted_iota(jnp.int32, (256, 512), 1)
        slots = wide_columns // 16 * 8 + wide_columns % 8
        hits = (lax.broadcasted_iota(jnp.int32, (256, 512), 0) == slots).astype(F32).astype(BF16)
        held = jnp.concatenate([order_lanes[0:1, :], order_lanes[1:2, :]], axis=1).astype(F32)
        held = jnp.broadcast_to(held, (8, 256))
        high = jnp.floor(held * (1 / 32))
        low = held - 32.0 * high
        row = 32.0 * jnp.dot(high.astype(BF16), hits, preferred_element_type=F32)
        return (row + jnp.dot(low.astype(BF16), hits, preferred_element_type=F32))[0:1, :]

    def slope_rows(m_row):
        quarter = jnp.where(columns % 16 >= 8, N_PHI / 4, 0.0)
        cos_b, sin_b = waves(lax.broadcasted_iota(jnp.int32, (64, 512), 0).astype(F32) * m_row)
        tb[0] = cos_b
        tb[1] = sin_b
        scaled = m_row * (1.0 / N_DEG)

        def rows(a, carry):
            cos_a, sin_a = waves((64 * a).astype(F32) * m_row + quarter)
            sines = sin_a * tb[0] + cos_a * tb[1]
            slope_t[pl.ds(pl.multiple_of(64 * a, 64), 64), :] = (-(scaled * sines)).astype(BF16)
            return carry

        lax.fori_loop(0, N_PHI // 64, rows, 0)

    def fourier_rows(m_row):
        macc[:, :128] = jnp.transpose(jnp.broadcast_to(m_row, (128, 512)))
        lanes = lax.broadcasted_iota(jnp.int32, (64, 128), 1).astype(F32)
        second = lax.broadcasted_iota(jnp.int32, (64, 128), 0) % 16 >= 8
        quarter = jnp.where(second, N_PHI / 4, 0.0)

        def rows_of(block, carry):
            rows = pl.ds(pl.multiple_of(64 * block, 64), 64)
            m = macc[rows, :128]
            cos_b, sin_b = waves(lanes * m)
            cos_a, sin_a = waves(jnp.minimum(lanes, N_PHI // 128 - 1) * 128.0 * m + quarter)
            for a in range(N_PHI // 128):
                cosines = cos_a[:, a : a + 1] * cos_b - sin_a[:, a : a + 1] * sin_b
                fourier_t[rows, 128 * a : 128 * a + 128] = cosines.astype(BF16)
            return carry

        lax.fori_loop(0, 8, rows_of, 0)

    def turn_flow(block, carry):
        raw_copy(block).wait()
        piece = r2send[block % 4 // 2, block % 2].reshape(2, 1024, 128)
        for half in range(2):
            wide[half] = piece[half].astype(F32)

        @pl.when(block + 4 < N_PHI // FB)
        def _():
            raw_copy(block + 4).start()

        for half in range(2):
            rows = pl.ds(pl.multiple_of(FB * block + 64 * half, 64), 64)
            for level in range(16):
                fl[level, rows, :] = wide[half, pl.ds(level, 64, stride=16), :].astype(BF16)
        return carry

    def prepare(slot, carry):
        order = orders[16 * lat + 8 * c + slot]
        weights = jnp.concatenate([qw[pl.ds(2 * y, 1), :], qw[pl.ds(2 * y + 1, 1), :]], axis=1)
        for quarter in range(4):
            block = jnp.transpose(lg[slot, :, 256 * quarter : 256 * quarter + 256].astype(F32))
            degrees = lax.broadcasted_iota(jnp.int32, block.shape, 0) + 256 * quarter
            block = jnp.where(degrees >= order, block, 0.0)
            lg[slot, :, 256 * quarter : 256 * quarter + 256] = block.astype(BF16)
            rows = pl.ds(pl.multiple_of(256 * ((quarter - y + 4) % 4), 256), 256)
            wt[slot, rows, :] = (block * weights).astype(BF16)
        return carry

    def synthesize(j):
        gather_rest(j)
        lanes = pl.ds(pl.multiple_of(256 * y, 256), 256)
        eye = (
            lax.broadcasted_iota(jnp.int32, (256, 256), 0)
            == lax.broadcasted_iota(jnp.int32, (256, 256), 1)
        ).astype(F32).astype(BF16)

        def one(slot, carry):
            values = jnp.zeros((128, 256), F32)
            for quarter in range(4):
                span = pl.ds(256 * quarter, 256)
                values += jnp.dot(
                    ef[j, :, slot, :, span].reshape(128, 256), lg[slot, :, span],
                    preferred_element_type=F32,
                )
            own = ef[j, :, slot, :, lanes].astype(F32)
            own = jnp.concatenate([own[:, :8], own[:, 8:]], axis=0).reshape(128, 256)
            pre[j, slot] = lax.dot_general(
                eye, own.astype(BF16), NT, preferred_element_type=F32
            ).astype(BF16)
            for block in range(8):
                for part in range(2):
                    at = 16 * block + 8 * part
                    for core in range(2):
                        wide[core, pl.ds(128 * block + 8 * part + slot, 8, stride=16), :] = values[
                            at : at + 8, 128 * core : 128 * core + 128
                        ]
            return carry

        lax.fori_loop(0, 8, one, 0)
        buf = j % 2
        if j >= 2:
            sent(gsend.at[buf], g_send.at[j - 2])

        def pack(p, carry):
            rows = pl.ds(pl.multiple_of(64 * p, 64), 64)
            for core in range(2):
                gsend[buf, 2 * p + core] = wide[core, rows, :].astype(BF16).reshape(4, 16, 128)
            return carry

        lax.fori_loop(0, 16, pack, 0)
        all_to_all(
            lambda dest: gsend.at[buf, dest], grecv.at[j, :, pl.ds(16 * me, 16), :],
            g_send.at[j], g_recv.at[j],
        )

    def grid(j):
        wait_bytes(grecv.at[j], g_recv.at[j])
        buf = j % 2
        if j >= 2:
            sent(msend.at[buf], m_send.at[j - 2])

        macc[...] = jnp.zeros_like(macc)

        def longitudes(kb, carry):
            rows = pl.ds(pl.multiple_of(KB * kb, KB), KB)
            points = jnp.concatenate([grecv[j, i] for i in range(4)], axis=1)
            slope = jnp.dot(slope_t[rows, :], points, preferred_element_type=F32)
            speed = jnp.concatenate([fl[4 * j + i, rows, :] for i in range(4)], axis=1)
            forcing = (-speed.astype(F32) * slope).astype(BF16)
            macc[...] += jnp.dot(fourier_t[:, rows], forcing, preferred_element_type=F32)
            return carry

        lax.fori_loop(0, N_PHI // KB, longitudes, 0)
        for i in range(4):
            done = (macc[:, 128 * i : 128 * i + 128] * (2.0 / N_PHI)).astype(BF16)
            msend[buf, :, i] = done.reshape(PEERS, 16, 128)
        all_to_all(
            lambda dest: msend.at[buf, dest], mrecv.at[j, me], m_send.at[j], m_recv.at[j]
        )

    def arrange(j):
        wait_bytes(mrecv.at[j], m_recv.at[j])

        def unpack(p, carry):
            rows = pl.ds(pl.multiple_of(64 * p, 64), 64)
            for core in range(2):
                wide[core, rows, :] = mrecv[j, 2 * p + core].reshape(64, 128).astype(F32)
            return carry

        lax.fori_loop(0, 16, unpack, 0)

        def one(slot, carry):
            for part in range(2):
                for block in range(0, 8, 2):
                    tiles = [
                        [
                            wide[core, pl.ds(128 * (block + q) + 8 * part + slot, 8, stride=16), :]
                            for core in range(2)
                        ]
                        for q in range(2)
                    ]
                    both = jnp.concatenate(
                        [jnp.concatenate(pieces, axis=1) for pieces in tiles], axis=0
                    )
                    at = 64 * part + 8 * block
                    mx[slot, at : at + 16, :] = both.astype(BF16)
            return carry

        lax.fori_loop(0, 8, one, 0)

    def reduce_first(j):
        buf = j % 2
        if j >= 2:
            wait_bytes(r1send.at[buf], r1_ssem.at[j - 2])
            wait_bytes(r2send.at[buf], r2_ssem.at[j - 2])

        def foreign(slot, carry):
            sums = lax.dot_general(wt[slot], mx[slot], NT, preferred_element_type=F32)
            rows = pl.ds(pl.multiple_of(256 * slot, 256), 256)
            own = sums[:256] + pre[j, slot].astype(F32)
            pre[j, slot], fl[4 * j, rows, :] = halves(own)
            r2send[buf, 0, slot], fl[4 * j + 1, rows, :] = halves(sums[256:512])
            r1send[buf, slot] = sums[512:768].astype(BF16)
            r2send[buf, 1, slot], fl[4 * j + 2, rows, :] = halves(sums[768:])
            return carry

        lax.fori_loop(0, 8, foreign, 0)
        for half, row in ((0, up), (1, down)):
            span = pl.ds(4 * half, 4)
            remote(
                r1send.at[buf, span], r1recv.at[j, span],
                r1_ssem.at[j], r1_rsem.at[j, half], (2 * row + c, lat),
            )
        for part in range(PARTS):
            reduce_send(j, 0, up, 1, part)
            reduce_send(j, 1, down, 0, part)

    def reduce_send(j, way, row, half, part):
        span, rows = pl.ds(4 * half, 4), pl.ds(ROWS * part, ROWS)
        remote(
            r2send.at[j % 2, way, span, rows, :], r2recv.at[j, way, span, rows, :],
            r2_ssem.at[j], r2_rsem.at[j, way, half, part], (2 * row + c, lat),
        )

    def reduce_second(j):
        for half in range(2):
            wait_bytes(r1recv.at[j, pl.ds(4 * half, 4)], r1_rsem.at[j, half])
        for part in range(PARTS):
            rows = pl.ds(ROWS * part, ROWS)
            for way, row, half in ((0, up, 0), (1, down, 1)):

                def near(slot, carry):
                    lows = pl.ds(pl.multiple_of(256 * slot + ROWS * part, ROWS), ROWS)
                    total = r2send[j % 2, way, slot, rows, :].astype(F32)
                    total += fl[4 * j + 1 + way, lows, :].astype(F32)
                    total += r1recv[j, slot, rows, :].astype(F32)
                    r2send[j % 2, way, slot, rows, :] = total.astype(BF16)
                    return carry

                lax.fori_loop(4 * half, 4 * half + 4, near, 0)
                reduce_send(j, way, row, half, part)

    def finish(j, part):
        buf, core, first = j % 2, part * 2 // PARTS, part % (PARTS // 2) * (32 // PARTS)
        rows = pl.ds(ROWS * part, ROWS)
        for way in range(2):
            for half in range(2):
                span = pl.ds(4 * half, 4)
                wait_bytes(r2recv.at[j, way, span, rows, :], r2_rsem.at[j, way, half, part])

        def one(slot, carry):
            lows = pl.ds(pl.multiple_of(256 * slot + ROWS * part, ROWS), ROWS)
            total = pre[j, slot, rows, :].astype(F32) + fl[4 * j, lows, :].astype(F32)
            total += r2recv[j, 0, slot, rows, :].astype(F32)
            total += r2recv[j, 1, slot, rows, :].astype(F32)
            for p in range(32 // PARTS):
                at = 64 * (first + p) + slot
                wide[core, pl.ds(at, 8, stride=8), :] = total[8 * p : 8 * p + 8]
            return carry

        lax.fori_loop(0, 8, one, 0)
        if j >= 2 and part == 0:
            sent(fsend.at[buf], f_send.at[j - 2])
            wait_bytes(fr.at[j - 2], f_recv.at[j - 2])

        def pack(p, carry):
            span = pl.ds(pl.multiple_of(64 * p, 64), 64)
            fsend[buf, 2 * p + core] = wide[core, span, :].astype(BF16)
            return carry

        lax.fori_loop(first, first + 32 // PARTS, pack, 0)

        def send(offset, carry):
            p = first + (lat + offset) % (32 // PARTS)
            itself = (p == lat) & (c == core)
            source, target = fsend.at[buf, 2 * p + core], fr.at[j, me]

            @pl.when(itself)
            def _():
                pltpu.make_async_copy(source, target, f_recv.at[j]).start()

            @pl.when(jnp.logical_not(itself))
            def _():
                remote(source, target, f_send.at[j], f_recv.at[j], (2 * y + core, p))

            return carry

        lax.fori_loop(0, 32 // PARTS, send, 0)

    def spread(degree, carry):
        source = lax.broadcasted_iota(jnp.int32, (256, 512), 0)
        lane = lax.broadcasted_iota(jnp.int32, (256, 512), 1)
        level = (lane % 64) // 4 * 16 + lane // 128 * 4 + lane % 4
        hits = (source == level).astype(F32).astype(BF16)
        lg[degree, :, :512] = jnp.dot(inv[degree], hits, preferred_element_type=F32).astype(BF16)
        return carry

    def out_copy(degree):
        return pltpu.make_async_copy(wt.at[degree, pl.ds(0, 512), :], out.at[degree], out_sem)

    def update(chunks, degree_pair, store):
        rows = pl.ds(pl.multiple_of(16 * degree_pair, 16), 16)
        width = 128 * len(chunks)
        part = lax.broadcasted_iota(jnp.int32, (256, width), 1) % 128 // 64
        pieces = [fr[j, :, rows, :].astype(F32) for j in chunks]
        for u in range(2):
            flat = [piece[:, 8 * u : 8 * u + 8, :].reshape(256, 128) for piece in pieces]
            left = jnp.concatenate(flat, axis=1)
            degree = 2 * degree_pair + u
            for half in range(2):
                right = lg[degree, :, 128 * chunks[0] : 128 * chunks[0] + width]
                store(degree, half, lax.dot_general(
                    jnp.where(part == half, left, 0.0).astype(BF16), right, NT,
                    preferred_element_type=F32,
                ))

    def early(degree_pair, carry):
        def store(degree, half, values):
            rows = pl.ds(pl.multiple_of(256 * degree, 256), 256)
            span = pl.ds(256 * half, 256)
            lg[degree, :, pl.ds(512 + 256 * half, 256)], slope_t[rows, span] = halves(values)

        update((0, 1, 2), degree_pair, store)
        return carry

    def late(degree_pair, carry):
        def store(degree, half, values):
            rows = pl.ds(pl.multiple_of(256 * degree, 256), 256)
            values += lg[degree, :, 512 + 256 * half : 768 + 256 * half].astype(F32)
            values += slope_t[rows, 256 * half : 256 * half + 256].astype(F32)
            wt[degree, 256 * half : 256 * half + 256, :] = values.astype(BF16)

        update((3,), degree_pair, store)
        for u in range(2):
            out_copy(2 * degree_pair + u).start()
        return carry

    def prepare_legendre():
        wait_bytes(lg, lg_recv)
        lax.fori_loop(0, 8, prepare, 0)

    def prepare_flow():
        lax.fori_loop(0, N_PHI // FB, turn_flow, 0)

    def prepare_tables():
        m_row = order_row()
        slope_rows(m_row)
        fourier_rows(m_row)

    def prepare_inverses():
        own_inverses.wait()
        lax.fori_loop(0, 8, spread, 0)

    def begin_radial():
        wait_bytes(fr.at[2], f_recv.at[2])
        lax.fori_loop(0, 4, early, 0)

    def swap_tables():
        mine = pl.ds(pl.multiple_of(128 * c, 128), 128)
        remote(
            leg.at[pl.ds(8 * (1 - c), 8)], lg.at[:, mine, :], lg_send, lg_recv,
            (2 * y + 1 - c, lat),
        )
        pltpu.make_async_copy(leg.at[pl.ds(8 * c, 8)], lg.at[:, mine, :], lg_recv).start()

    steps = dict(
        D=gather_direct, F=gather_forward, S=synthesize, G=grid, B=reduce_second,
        X=swap_tables, M=prepare_legendre, T=prepare_flow, P=prepare_tables,
        V=prepare_inverses, E=begin_radial, Z=finish,
    )
    for step in ORDER:
        if step[0] == "A":
            arrange(int(step[1]))
            reduce_first(int(step[1]))
        else:
            steps[step[0]](*(int(digit) for digit in step[1:]))

    for j in range(CHUNKS):
        wait_bytes(ef.at[j, pl.ds(0, 7)], ag_send.at[j])
    wait_bytes(lg.at[:, pl.ds(0, 128), :], lg_send)
    for j in range(CHUNKS - 2, CHUNKS):
        sent(gsend.at[j % 2], g_send.at[j])
        sent(msend.at[j % 2], m_send.at[j])
        wait_bytes(r1send.at[j % 2], r1_ssem.at[j])
        wait_bytes(r2send.at[j % 2], r2_ssem.at[j])
        sent(fsend.at[j % 2], f_send.at[j])
    wait_bytes(fr.at[3], f_recv.at[3])
    lax.fori_loop(0, 4, late, 0)
    wait_bytes(wt.at[:, pl.ds(0, 512), :], out_sem)


def shards(entropy, legendre, quad_weights, azimuthal_orders, azimuthal_flow, radial_inverses):
    ent = jnp.transpose(entropy, (0, 2, 3, 1)).reshape(16, 64, N_DEG)
    hbm = pl.BlockSpec(memory_space=pl.ANY)
    vmem = pl.BlockSpec(memory_space=pltpu.VMEM)
    smem = pl.BlockSpec(memory_space=pltpu.SMEM)
    dma = pltpu.SemaphoreType.DMA
    updated = pl.pallas_call(
        kernel,
        out_shape=jax.ShapeDtypeStruct((8, 512, 256), BF16),
        in_specs=[hbm, hbm, vmem, smem, vmem, hbm, hbm],
        out_specs=hbm,
        scratch_shapes=[
            pltpu.VMEM((16, 64, N_DEG), BF16),
            pltpu.VMEM((8, 256, 256), BF16),
            pltpu.VMEM((CHUNKS, PEERS, 64, 128), BF16),
            pltpu.VMEM((CHUNKS, 8, 8, 16, N_DEG), BF16),
            pltpu.VMEM((8, 256, N_DEG), BF16),
            pltpu.VMEM((8, N_DEG, 256), BF16),
            pltpu.VMEM((N_PHI, 512), BF16),
            pltpu.VMEM((512, N_PHI), BF16),
            pltpu.VMEM((16, N_PHI, 128), BF16),
            pltpu.VMEM((2, 64, 512), F32),
            pltpu.VMEM((2, PEERS, 4, 16, 128), BF16),
            pltpu.VMEM((CHUNKS, 4, 512, 128), BF16),
            pltpu.VMEM((2, PEERS, 4, 16, 128), BF16),
            pltpu.VMEM((CHUNKS, PEERS, 4, 16, 128), BF16),
            pltpu.VMEM((8, 128, 256), BF16),
            pltpu.VMEM((CHUNKS, 8, 256, 128), BF16),
            pltpu.VMEM((2, 1024, 128), F32),
            pltpu.VMEM((512, 512), F32),
            pltpu.VMEM((2, 8, 256, 128), BF16),
            pltpu.VMEM((CHUNKS, 8, 256, 128), BF16),
            pltpu.VMEM((2, 2, 8, 256, 128), BF16),
            pltpu.VMEM((CHUNKS, 2, 8, 256, 128), BF16),
            pltpu.VMEM((2, PEERS, 64, 128), BF16),
            dma((CHUNKS,)), dma((CHUNKS, 8)), dma, dma, dma((4,)),
            dma((CHUNKS,)), dma((CHUNKS,)), dma((CHUNKS,)), dma((CHUNKS,)),
            dma((CHUNKS,)), dma((CHUNKS, 2)), dma((CHUNKS,)), dma((CHUNKS, 2, 2, PARTS)),
            dma((CHUNKS,)), dma((CHUNKS,)), dma, dma, dma,
        ],
        compiler_params=pltpu.CompilerParams(
            collective_id=0, has_side_effects=True, vmem_limit_bytes=62 * 1024 * 1024
        ),
        cost_estimate=pl.CostEstimate(
            flops=17_000_000_000, bytes_accessed=24_000_000, transcendentals=0
        ),
    )(
        ent, legendre, quad_weights.reshape(8, 128), azimuthal_orders,
        azimuthal_orders.reshape(2, 128), azimuthal_flow.reshape(N_PHI // 16, 256, 128),
        radial_inverses,
    )
    return jnp.transpose(updated.reshape(8, 2, 256, 256), (2, 0, 1, 3))


def solution(mesh):
    placed = (
        P("lat", None, None, "rad"),
        P("lat", "rad", None),
        P(),
        P(),
        P(None, "lat", "rad"),
        P(("rad", "lat"), None, None),
    )
    return jax.shard_map(
        shards,
        mesh=mesh,
        in_specs=placed,
        out_specs=P(None, ("rad", "lat"), None, None),
        check_vma=False,
    )
```

```python
import math

import jax
import jax.numpy as jnp
from jax import lax
from jax.experimental import pallas as pl
from jax.experimental.pallas import tpu as pltpu
from jax.sharding import PartitionSpec as P

MESH = pl.DeviceIdType.MESH
F32, BF16 = jnp.float32, jnp.bfloat16
N_DEG = 1024
N_PHI = 3072
PEERS = 32
CHUNKS = 4
NT = (((1,), (1,)), ((), ()))
KB = 256
FB = 128
PARTS = 4
ROWS = 256 // PARTS
ORDER = (
    "D0", "X", "D1", "M", "F0", "T", "F1", "P", "S0", "D2", "D3", "S1", "G0", "F2", "G1", "F3",
    "A0", "S2", "S3", "A1", "B0", "G2", "B1", "G3", "V", "A2", "Z00", "Z01", "Z02", "Z03", "Z10",
    "Z11", "Z12", "Z13", "B2", "A3", "Z20", "Z21", "Z22", "Z23", "B3", "Z30", "Z31", "Z32", "Z33", "E",
)


def halves(values):
    high = values.astype(BF16)
    return high, (values - high.astype(F32)).astype(BF16)


def wait_bytes(ref, sem):
    pltpu.make_async_copy(ref, ref, sem).wait()


def waves(product):
    turns = jnp.floor(product * (4.0 / N_PHI) + 0.5)
    x = (product - turns * (N_PHI // 4)) * (2.0 * math.pi / N_PHI)
    x2 = x * x
    sine = x * (1.0 + x2 * (-1 / 6 + x2 * (1 / 120 + x2 * (-1 / 5040 + x2 * (1 / 362880)))))
    cosine = 1.0 + x2 * (-0.5 + x2 * (1 / 24 + x2 * (-1 / 720 + x2 * (1 / 40320))))
    quarter = turns - 4.0 * jnp.floor(turns * 0.25)
    odd = (quarter == 1.0) | (quarter == 3.0)
    first = jnp.where(odd, sine, cosine)
    second = jnp.where(odd, cosine, sine)
    cos = jnp.where((quarter == 1.0) | (quarter == 2.0), -first, first)
    sin = jnp.where(quarter >= 2.0, -second, second)
    return cos, sin


def kernel(
    ent, leg, qw, orders, order_lanes, flow, inverses, out,
    er, inv, fr, ef, lg, wt, slope_t, fourier_t, fl, tb, gsend, grecv, msend, mrecv, mx, pre, wide, macc,
    r1send, r1recv, r2send, r2recv, fsend,
    ag_send, ag_recv, lg_send, lg_recv, raw_sem, g_send, g_recv, m_send, m_recv,
    r1_ssem, r1_rsem, r2_ssem, r2_rsem, f_send, f_recv, er_sem, inv_sem, out_sem,
):
    rad = lax.axis_index("rad")
    lat = lax.axis_index("lat")
    y, c = rad // 2, rad % 2
    me = 2 * lat + c
    up, down, across = (y + 1) % 4, (y + 3) % 4, (y + 2) % 4

    def place(index):
        return (2 * y + index % 2, index // 2)

    def raw_copy(block):
        pieces = flow.at[pl.ds(FB // 16 * block, FB // 16)]
        place = r2send.at[block % 4 // 2, block % 2]
        return pltpu.make_async_copy(pieces, place, raw_sem.at[block % 4])

    own_rows = pltpu.make_async_copy(ent, er, er_sem)
    own_rows.start()
    for block in range(4):
        raw_copy(block).start()
    own_inverses = pltpu.make_async_copy(inverses, inv, inv_sem)
    own_inverses.start()

    barrier = pltpu.get_barrier_semaphore()

    def greet(offset, carry):
        pl.semaphore_signal(
            barrier, inc=1, device_id=place((me + offset) % PEERS), device_id_type=MESH
        )
        return carry

    lax.fori_loop(1, PEERS, greet, 0)
    for row in (up, down):
        for core in range(2):
            pl.semaphore_signal(
                barrier, inc=1, device_id=(2 * row + core, lat), device_id_type=MESH
            )

    def regroup(slot, carry):
        rows = er[slot].astype(F32).reshape(4, 16, N_DEG)
        low = lax.broadcasted_iota(jnp.int32, (8, N_DEG), 0) < 4
        for j in range(CHUNKS):
            tiles = []
            for part in range(2):
                first = rows[2 * part, 8 * (j // 2) : 8 * (j // 2) + 8]
                second = rows[2 * part + 1, 8 * (j // 2) : 8 * (j // 2) + 8]
                if j % 2 == 0:
                    tiles.append(jnp.where(low, first, pltpu.roll(second, 4, axis=0)))
                else:
                    tiles.append(jnp.where(low, pltpu.roll(first, 4, axis=0), second))
            er[slot, 16 * j : 16 * j + 16, :] = jnp.concatenate(tiles, axis=0).astype(BF16)
        return carry

    own_rows.wait()
    lax.fori_loop(0, 16, regroup, 0)
    pl.semaphore_wait(barrier, PEERS - 1 + 4)

    def remote(src, dst, send_sem, recv_sem, device):
        pltpu.make_async_remote_copy(
            src_ref=src, dst_ref=dst, send_sem=send_sem, recv_sem=recv_sem,
            device_id=device, device_id_type=MESH,
        ).start()

    def all_to_all(source, target, send_sem, recv_sem):
        pltpu.make_async_copy(source(me), target, recv_sem).start()

        def send(offset, carry):
            dest = (me + offset) % PEERS
            remote(source(dest), target, send_sem, recv_sem, place(dest))
            return carry

        lax.fori_loop(1, PEERS, send, 0)

    def sent(buffer, sem):
        wait_bytes(buffer.at[pl.ds(0, PEERS - 1)], sem)

    def gather_direct(j):
        rows = pl.ds(16 * j, 16)
        for row in (up, down):
            for core in range(2):
                remote(
                    er.at[pl.ds(8 * core, 8), rows, :], ef.at[j, rad],
                    ag_send.at[j], ag_recv.at[j, rad], (2 * row + core, lat),
                )
        remote(
            er.at[pl.ds(8 * (1 - c), 8), rows, :], ef.at[j, rad],
            ag_send.at[j], ag_recv.at[j, rad], (2 * y + 1 - c, lat),
        )
        pltpu.make_async_copy(
            er.at[pl.ds(8 * c, 8), rows, :], ef.at[j, rad], ag_recv.at[j, rad]
        ).start()

    def gather_wait(j, block):
        wait_bytes(ef.at[j, block], ag_recv.at[j, block])

    def gather_forward(j):
        for block, row in ((2 * down, up), (2 * up + 1, down)):
            gather_wait(j, block)
            remote(
                ef.at[j, block], ef.at[j, block],
                ag_send.at[j], ag_recv.at[j, block], (2 * row + c, lat),
            )

    def gather_rest(j):
        for block in (rad, 2 * y + 1 - c, 2 * down + 1, 2 * up, 2 * across, 2 * across + 1):
            gather_wait(j, block)

    columns = lax.broadcasted_iota(jnp.int32, (1, 512), 1)

    def order_row():
        wide_columns = lax.broadcasted_iota(jnp.int32, (256, 512), 1)
        slots = wide_columns // 16 * 8 + wide_columns % 8
        hits = (lax.broadcasted_iota(jnp.int32, (256, 512), 0) == slots).astype(F32).astype(BF16)
        held = jnp.concatenate([order_lanes[0:1, :], order_lanes[1:2, :]], axis=1).astype(F32)
        held = jnp.broadcast_to(held, (8, 256))
        high = jnp.floor(held * (1 / 32))
        low = held - 32.0 * high
        row = 32.0 * jnp.dot(high.astype(BF16), hits, preferred_element_type=F32)
        return (row + jnp.dot(low.astype(BF16), hits, preferred_element_type=F32))[0:1, :]

    def slope_rows(m_row):
        quarter = jnp.where(columns % 16 >= 8, N_PHI / 4, 0.0)
        cos_b, sin_b = waves(lax.broadcasted_iota(jnp.int32, (64, 512), 0).astype(F32) * m_row)
        tb[0] = cos_b
        tb[1] = sin_b
        scaled = m_row * (1.0 / N_DEG)

        def rows(a, carry):
            cos_a, sin_a = waves((64 * a).astype(F32) * m_row + quarter)
            sines = sin_a * tb[0] + cos_a * tb[1]
            slope_t[pl.ds(pl.multiple_of(64 * a, 64), 64), :] = (-(scaled * sines)).astype(BF16)
            return carry

        lax.fori_loop(0, N_PHI // 64, rows, 0)

    def fourier_rows(m_row):
        macc[:, :128] = jnp.transpose(jnp.broadcast_to(m_row, (128, 512)))
        lanes = lax.broadcasted_iota(jnp.int32, (64, 128), 1).astype(F32)
        second = lax.broadcasted_iota(jnp.int32, (64, 128), 0) % 16 >= 8
        quarter = jnp.where(second, N_PHI / 4, 0.0)

        def rows_of(block, carry):
            rows = pl.ds(pl.multiple_of(64 * block, 64), 64)
            m = macc[rows, :128]
            cos_b, sin_b = waves(lanes * m)
            cos_a, sin_a = waves(jnp.minimum(lanes, N_PHI // 128 - 1) * 128.0 * m + quarter)
            for a in range(N_PHI // 128):
                cosines = cos_a[:, a : a + 1] * cos_b - sin_a[:, a : a + 1] * sin_b
                fourier_t[rows, 128 * a : 128 * a + 128] = cosines.astype(BF16)
            return carry

        lax.fori_loop(0, 8, rows_of, 0)

    def turn_flow(block, carry):
        raw_copy(block).wait()
        piece = r2send[block % 4 // 2, block % 2].reshape(2, 1024, 128)
        for half in range(2):
            wide[half] = piece[half].astype(F32)

        @pl.when(block + 4 < N_PHI // FB)
        def _():
            raw_copy(block + 4).start()

        for half in range(2):
            rows = pl.ds(pl.multiple_of(FB * block + 64 * half, 64), 64)
            for level in range(16):
                fl[level, rows, :] = wide[half, pl.ds(level, 64, stride=16), :].astype(BF16)
        return carry

    def prepare(slot, carry):
        order = orders[16 * lat + 8 * c + slot]
        weights = jnp.concatenate([qw[pl.ds(2 * y, 1), :], qw[pl.ds(2 * y + 1, 1), :]], axis=1)
        for quarter in range(4):
            block = jnp.transpose(lg[slot, :, 256 * quarter : 256 * quarter + 256].astype(F32))
            degrees = lax.broadcasted_iota(jnp.int32, block.shape, 0) + 256 * quarter
            block = jnp.where(degrees >= order, block, 0.0)
            lg[slot, :, 256 * quarter : 256 * quarter + 256] = block.astype(BF16)
            rows = pl.ds(pl.multiple_of(256 * ((quarter - y + 4) % 4), 256), 256)
            wt[slot, rows, :] = (block * weights).astype(BF16)
        return carry

    def synthesize(j):
        gather_rest(j)
        lanes = pl.ds(pl.multiple_of(256 * y, 256), 256)
        eye = (
            lax.broadcasted_iota(jnp.int32, (256, 256), 0)
            == lax.broadcasted_iota(jnp.int32, (256, 256), 1)
        ).astype(F32).astype(BF16)

        def one(slot, carry):
            values = jnp.zeros((128, 256), F32)
            for quarter in range(4):
                span = pl.ds(256 * quarter, 256)
                values += jnp.dot(
                    ef[j, :, slot, :, span].reshape(128, 256), lg[slot, :, span],
                    preferred_element_type=F32,
                )
            own = ef[j, :, slot, :, lanes].astype(F32)
            own = jnp.concatenate([own[:, :8], own[:, 8:]], axis=0).reshape(128, 256)
            pre[j, slot] = lax.dot_general(
                eye, own.astype(BF16), NT, preferred_element_type=F32
            ).astype(BF16)
            for block in range(8):
                for part in range(2):
                    at = 16 * block + 8 * part
                    for core in range(2):
                        wide[core, pl.ds(128 * block + 8 * part + slot, 8, stride=16), :] = values[
                            at : at + 8, 128 * core : 128 * core + 128
                        ]
            return carry

        lax.fori_loop(0, 8, one, 0)
        buf = j % 2
        if j >= 2:
            sent(gsend.at[buf], g_send.at[j - 2])

        def pack(p, carry):
            rows = pl.ds(pl.multiple_of(64 * p, 64), 64)
            for core in range(2):
                gsend[buf, 2 * p + core] = wide[core, rows, :].astype(BF16).reshape(4, 16, 128)
            return carry

        lax.fori_loop(0, 16, pack, 0)
        all_to_all(
            lambda dest: gsend.at[buf, dest], grecv.at[j, :, pl.ds(16 * me, 16), :],
            g_send.at[j], g_recv.at[j],
        )

    def grid(j):
        wait_bytes(grecv.at[j], g_recv.at[j])
        buf = j % 2
        if j >= 2:
            sent(msend.at[buf], m_send.at[j - 2])

        macc[...] = jnp.zeros_like(macc)

        def longitudes(kb, carry):
            rows = pl.ds(pl.multiple_of(KB * kb, KB), KB)
            points = jnp.concatenate([grecv[j, i] for i in range(4)], axis=1)
            slope = jnp.dot(slope_t[rows, :], points, preferred_element_type=F32)
            speed = jnp.concatenate([fl[4 * j + i, rows, :] for i in range(4)], axis=1)
            forcing = (-speed.astype(F32) * slope).astype(BF16)
            macc[...] += jnp.dot(fourier_t[:, rows], forcing, preferred_element_type=F32)
            return carry

        lax.fori_loop(0, N_PHI // KB, longitudes, 0)
        for i in range(4):
            done = (macc[:, 128 * i : 128 * i + 128] * (2.0 / N_PHI)).astype(BF16)
            msend[buf, :, i] = done.reshape(PEERS, 16, 128)
        all_to_all(
            lambda dest: msend.at[buf, dest], mrecv.at[j, me], m_send.at[j], m_recv.at[j]
        )

    def arrange(j):
        wait_bytes(mrecv.at[j], m_recv.at[j])

        def unpack(p, carry):
            rows = pl.ds(pl.multiple_of(64 * p, 64), 64)
            for core in range(2):
                wide[core, rows, :] = mrecv[j, 2 * p + core].reshape(64, 128).astype(F32)
            return carry

        lax.fori_loop(0, 16, unpack, 0)

        def one(slot, carry):
            for part in range(2):
                for block in range(0, 8, 2):
                    tiles = [
                        [
                            wide[core, pl.ds(128 * (block + q) + 8 * part + slot, 8, stride=16), :]
                            for core in range(2)
                        ]
                        for q in range(2)
                    ]
                    both = jnp.concatenate(
                        [jnp.concatenate(pieces, axis=1) for pieces in tiles], axis=0
                    )
                    at = 64 * part + 8 * block
                    mx[slot, at : at + 16, :] = both.astype(BF16)
            return carry

        lax.fori_loop(0, 8, one, 0)

    def reduce_first(j):
        buf = j % 2
        if j >= 2:
            wait_bytes(r1send.at[buf], r1_ssem.at[j - 2])
            wait_bytes(r2send.at[buf], r2_ssem.at[j - 2])

        def foreign(slot, carry):
            sums = lax.dot_general(wt[slot], mx[slot], NT, preferred_element_type=F32)
            rows = pl.ds(pl.multiple_of(256 * slot, 256), 256)
            own = sums[:256] + pre[j, slot].astype(F32)
            pre[j, slot], fl[4 * j, rows, :] = halves(own)
            r2send[buf, 0, slot], fl[4 * j + 1, rows, :] = halves(sums[256:512])
            r1send[buf, slot] = sums[512:768].astype(BF16)
            r2send[buf, 1, slot], fl[4 * j + 2, rows, :] = halves(sums[768:])
            return carry

        lax.fori_loop(0, 8, foreign, 0)
        for half, row in ((0, up), (1, down)):
            span = pl.ds(4 * half, 4)
            remote(
                r1send.at[buf, span], r1recv.at[j, span],
                r1_ssem.at[j], r1_rsem.at[j, half], (2 * row + c, lat),
            )
        for part in range(PARTS):
            reduce_send(j, 0, up, 1, part)
            reduce_send(j, 1, down, 0, part)

    def reduce_send(j, way, row, half, part):
        span, rows = pl.ds(4 * half, 4), pl.ds(ROWS * part, ROWS)
        remote(
            r2send.at[j % 2, way, span, rows, :], r2recv.at[j, way, span, rows, :],
            r2_ssem.at[j], r2_rsem.at[j, way, half, part], (2 * row + c, lat),
        )

    def reduce_second(j):
        for half in range(2):
            wait_bytes(r1recv.at[j, pl.ds(4 * half, 4)], r1_rsem.at[j, half])
        for part in range(PARTS):
            rows = pl.ds(ROWS * part, ROWS)
            for way, row, half in ((0, up, 0), (1, down, 1)):

                def near(slot, carry):
                    lows = pl.ds(pl.multiple_of(256 * slot + ROWS * part, ROWS), ROWS)
                    total = r2send[j % 2, way, slot, rows, :].astype(F32)
                    total += fl[4 * j + 1 + way, lows, :].astype(F32)
                    total += r1recv[j, slot, rows, :].astype(F32)
                    r2send[j % 2, way, slot, rows, :] = total.astype(BF16)
                    return carry

                lax.fori_loop(4 * half, 4 * half + 4, near, 0)
                reduce_send(j, way, row, half, part)

    def finish(j, part):
        buf, core, first = j % 2, part * 2 // PARTS, part % (PARTS // 2) * (32 // PARTS)
        rows = pl.ds(ROWS * part, ROWS)
        for way in range(2):
            for half in range(2):
                span = pl.ds(4 * half, 4)
                wait_bytes(r2recv.at[j, way, span, rows, :], r2_rsem.at[j, way, half, part])

        def one(slot, carry):
            lows = pl.ds(pl.multiple_of(256 * slot + ROWS * part, ROWS), ROWS)
            total = pre[j, slot, rows, :].astype(F32) + fl[4 * j, lows, :].astype(F32)
            total += r2recv[j, 0, slot, rows, :].astype(F32)
            total += r2recv[j, 1, slot, rows, :].astype(F32)
            for p in range(32 // PARTS):
                at = 64 * (first + p) + slot
                wide[core, pl.ds(at, 8, stride=8), :] = total[8 * p : 8 * p + 8]
            return carry

        lax.fori_loop(0, 8, one, 0)
        if j >= 2 and part == 0:
            sent(fsend.at[buf], f_send.at[j - 2])
            wait_bytes(fr.at[j - 2], f_recv.at[j - 2])

        def pack(p, carry):
            span = pl.ds(pl.multiple_of(64 * p, 64), 64)
            fsend[buf, 2 * p + core] = wide[core, span, :].astype(BF16)
            return carry

        lax.fori_loop(first, first + 32 // PARTS, pack, 0)

        def send(offset, carry):
            p = first + (lat + offset) % (32 // PARTS)
            itself = (p == lat) & (c == core)
            source, target = fsend.at[buf, 2 * p + core], fr.at[j, me]

            @pl.when(itself)
            def _():
                pltpu.make_async_copy(source, target, f_recv.at[j]).start()

            @pl.when(jnp.logical_not(itself))
            def _():
                remote(source, target, f_send.at[j], f_recv.at[j], (2 * y + core, p))

            return carry

        lax.fori_loop(0, 32 // PARTS, send, 0)

    def spread(degree, carry):
        source = lax.broadcasted_iota(jnp.int32, (256, 512), 0)
        lane = lax.broadcasted_iota(jnp.int32, (256, 512), 1)
        level = (lane % 64) // 4 * 16 + lane // 128 * 4 + lane % 4
        hits = (source == level).astype(F32).astype(BF16)
        lg[degree, :, :512] = jnp.dot(inv[degree], hits, preferred_element_type=F32).astype(BF16)
        return carry

    def out_copy(degree):
        return pltpu.make_async_copy(wt.at[degree, pl.ds(0, 512), :], out.at[degree], out_sem)

    def update(chunks, degree_pair, store):
        rows = pl.ds(pl.multiple_of(16 * degree_pair, 16), 16)
        width = 128 * len(chunks)
        part = lax.broadcasted_iota(jnp.int32, (256, width), 1) % 128 // 64
        pieces = [fr[j, :, rows, :].astype(F32) for j in chunks]
        for u in range(2):
            flat = [piece[:, 8 * u : 8 * u + 8, :].reshape(256, 128) for piece in pieces]
            left = jnp.concatenate(flat, axis=1)
            degree = 2 * degree_pair + u
            for half in range(2):
                right = lg[degree, :, 128 * chunks[0] : 128 * chunks[0] + width]
                store(degree, half, lax.dot_general(
                    jnp.where(part == half, left, 0.0).astype(BF16), right, NT,
                    preferred_element_type=F32,
                ))

    def early(degree_pair, carry):
        def store(degree, half, values):
            rows = pl.ds(pl.multiple_of(256 * degree, 256), 256)
            span = pl.ds(256 * half, 256)
            lg[degree, :, pl.ds(512 + 256 * half, 256)], slope_t[rows, span] = halves(values)

        update((0, 1, 2), degree_pair, store)
        return carry

    def late(degree_pair, carry):
        def store(degree, half, values):
            rows = pl.ds(pl.multiple_of(256 * degree, 256), 256)
            values += lg[degree, :, 512 + 256 * half : 768 + 256 * half].astype(F32)
            values += slope_t[rows, 256 * half : 256 * half + 256].astype(F32)
            wt[degree, 256 * half : 256 * half + 256, :] = values.astype(BF16)

        update((3,), degree_pair, store)
        for u in range(2):
            out_copy(2 * degree_pair + u).start()
        return carry

    def prepare_legendre():
        wait_bytes(lg, lg_recv)
        lax.fori_loop(0, 8, prepare, 0)

    def prepare_flow():
        lax.fori_loop(0, N_PHI // FB, turn_flow, 0)

    def prepare_tables():
        m_row = order_row()
        slope_rows(m_row)
        fourier_rows(m_row)

    def prepare_inverses():
        own_inverses.wait()
        lax.fori_loop(0, 8, spread, 0)

    def begin_radial():
        wait_bytes(fr.at[2], f_recv.at[2])
        lax.fori_loop(0, 4, early, 0)

    def swap_tables():
        mine = pl.ds(pl.multiple_of(128 * c, 128), 128)
        remote(
            leg.at[pl.ds(8 * (1 - c), 8)], lg.at[:, mine, :], lg_send, lg_recv,
            (2 * y + 1 - c, lat),
        )
        pltpu.make_async_copy(leg.at[pl.ds(8 * c, 8)], lg.at[:, mine, :], lg_recv).start()

    steps = dict(
        D=gather_direct, F=gather_forward, S=synthesize, G=grid, B=reduce_second,
        X=swap_tables, M=prepare_legendre, T=prepare_flow, P=prepare_tables,
        V=prepare_inverses, E=begin_radial, Z=finish,
    )
    for step in ORDER:
        if step[0] == "A":
            arrange(int(step[1]))
            reduce_first(int(step[1]))
        else:
            steps[step[0]](*(int(digit) for digit in step[1:]))

    for j in range(CHUNKS):
        wait_bytes(ef.at[j, pl.ds(0, 7)], ag_send.at[j])
    wait_bytes(lg.at[:, pl.ds(0, 128), :], lg_send)
    for j in range(CHUNKS - 2, CHUNKS):
        sent(gsend.at[j % 2], g_send.at[j])
        sent(msend.at[j % 2], m_send.at[j])
        wait_bytes(r1send.at[j % 2], r1_ssem.at[j])
        wait_bytes(r2send.at[j % 2], r2_ssem.at[j])
        sent(fsend.at[j % 2], f_send.at[j])
    wait_bytes(fr.at[3], f_recv.at[3])
    lax.fori_loop(0, 4, late, 0)
    wait_bytes(wt.at[:, pl.ds(0, 512), :], out_sem)


def shards(entropy, legendre, quad_weights, azimuthal_orders, azimuthal_flow, radial_inverses):
    ent = jnp.transpose(entropy, (0, 2, 3, 1)).reshape(16, 64, N_DEG)
    hbm = pl.BlockSpec(memory_space=pl.ANY)
    vmem = pl.BlockSpec(memory_space=pltpu.VMEM)
    smem = pl.BlockSpec(memory_space=pltpu.SMEM)
    dma = pltpu.SemaphoreType.DMA
    updated = pl.pallas_call(
        kernel,
        out_shape=jax.ShapeDtypeStruct((8, 512, 256), BF16),
        in_specs=[hbm, hbm, vmem, smem, vmem, hbm, hbm],
        out_specs=hbm,
        scratch_shapes=[
            pltpu.VMEM((16, 64, N_DEG), BF16),
            pltpu.VMEM((8, 256, 256), BF16),
            pltpu.VMEM((CHUNKS, PEERS, 64, 128), BF16),
            pltpu.VMEM((CHUNKS, 8, 8, 16, N_DEG), BF16),
            pltpu.VMEM((8, 256, N_DEG), BF16),
            pltpu.VMEM((8, N_DEG, 256), BF16),
            pltpu.VMEM((N_PHI, 512), BF16),
            pltpu.VMEM((512, N_PHI), BF16),
            pltpu.VMEM((16, N_PHI, 128), BF16),
            pltpu.VMEM((2, 64, 512), F32),
            pltpu.VMEM((2, PEERS, 4, 16, 128), BF16),
            pltpu.VMEM((CHUNKS, 4, 512, 128), BF16),
            pltpu.VMEM((2, PEERS, 4, 16, 128), BF16),
            pltpu.VMEM((CHUNKS, PEERS, 4, 16, 128), BF16),
            pltpu.VMEM((8, 128, 256), BF16),
            pltpu.VMEM((CHUNKS, 8, 256, 128), BF16),
            pltpu.VMEM((2, 1024, 128), F32),
            pltpu.VMEM((512, 512), F32),
            pltpu.VMEM((2, 8, 256, 128), BF16),
            pltpu.VMEM((CHUNKS, 8, 256, 128), BF16),
            pltpu.VMEM((2, 2, 8, 256, 128), BF16),
            pltpu.VMEM((CHUNKS, 2, 8, 256, 128), BF16),
            pltpu.VMEM((2, PEERS, 64, 128), BF16),
            dma((CHUNKS,)), dma((CHUNKS, 8)), dma, dma, dma((4,)),
            dma((CHUNKS,)), dma((CHUNKS,)), dma((CHUNKS,)), dma((CHUNKS,)),
            dma((CHUNKS,)), dma((CHUNKS, 2)), dma((CHUNKS,)), dma((CHUNKS, 2, 2, PARTS)),
            dma((CHUNKS,)), dma((CHUNKS,)), dma, dma, dma,
        ],
        compiler_params=pltpu.CompilerParams(
            collective_id=0, has_side_effects=True, vmem_limit_bytes=62 * 1024 * 1024
        ),
        cost_estimate=pl.CostEstimate(
            flops=17_000_000_000, bytes_accessed=24_000_000, transcendentals=0
        ),
    )(
        ent, legendre, quad_weights.reshape(8, 128), azimuthal_orders,
        azimuthal_orders.reshape(2, 128), azimuthal_flow.reshape(N_PHI // 16, 256, 128),
        radial_inverses,
    )
    return jnp.transpose(updated.reshape(8, 2, 256, 256), (2, 0, 1, 3))


def solution(mesh):
    placed = (
        P("lat", None, None, "rad"),
        P("lat", "rad", None),
        P(),
        P(),
        P(None, "lat", "rad"),
        P(("rad", "lat"), None, None),
    )
    return jax.shard_map(
        shards,
        mesh=mesh,
        in_specs=placed,
        out_specs=P(None, ("rad", "lat"), None, None),
        check_vma=False,
    )
```
